256 devices in a mesh: dp: 32 (over z, x), tensor: 8 (over y, core).
Axes of the slice: x: 4, y: 4, z: 8, core: 2. Of those that a mesh axis runs over, the one named last changes fastest.
Arguments:
- queries: bfloat16 [8192, 3072], P('dp', 'tensor'), may hold values from -100 to 100
- keys: bfloat16 [8192, 3072], P('dp', 'tensor'), may hold values from -8 to 8
- values: bfloat16 [8192, 3072], P('dp', 'tensor'), may hold values from -6 to 6
- upstream: bfloat16 [8192, 6144], P('dp', 'tensor'), may hold values from -6 to 6
- out_weight: bfloat16 [6144, 3072], P('dp', 'tensor'), may hold values from -0.109375 to 0.109375
- fisher: float32 [6144, 3072], P('dp', 'tensor'), may hold values from 0.02 to 0.2
- image_lengths: int32 [32, 8], P('dp'), may hold values from 1 to 128, as said below
Outputs:
- grad_queries: bfloat16 [8192, 3072], P('dp', 'tensor')
- grad_keys: bfloat16 [8192, 3072], P('dp', 'tensor')
- grad_values: bfloat16 [8192, 3072], P('dp', 'tensor')
- weight_grad: float32 [6144, 3072], P('dp', 'tensor')
- fisher_next: float32 [6144, 3072], P('dp', 'tensor')
The draws below stay inside these ranges and needn't reach their ends.
Inputs may be any that keep to these rules, and one draw needn't show every extreme that they name: `image_lengths`: each row lists the patch counts of 8 images packed one after another from the first slot of a sequence; a row sums to at most 256, and in every draw some row sums to exactly 256. No image has more than 128 patches, and in every draw some image has exactly that many.
All inputs are finite; a program needn't handle non-finite values.
Results may differ from the reference program's by a relative error of at most 0.028.
Values may be sent and summed in bfloat16 or wider, within the bound.
A program may use at most 64 MiB of HBM per device.

```python
import math
import jax
import jax.numpy as jnp
from jax import lax

D = 6144
H = 24
HD = 128
IMGS = 8
TOK_DEV = 256
TOKENS = 8192
HL = 3072
N_DP = 32


def paired_fields(key):
    part_query, part_key = jax.random.split(key, 2)
    base_keys = jax.random.normal(part_key, (TOKENS, HL), jnp.float32)
    base_queries = jax.random.normal(part_query, (TOKENS, HL), jnp.float32)
    keys_out = base_keys
    queries_out = base_queries
    return (jnp.clip(queries_out, -100.0, 100.0), jnp.clip(keys_out, -8.0, 8.0))


def draw_queries(key, part):
    fields = paired_fields(key)
    return fields[0].astype(jnp.bfloat16)


def draw_keys(key, part):
    fields = paired_fields(key)
    return fields[1].astype(jnp.bfloat16)


def split_counts(totals, shares):
    spare = totals - shares.shape[1]
    running = jnp.cumsum(shares, axis=1)
    bounds = spare[:, None] * running // running[:, -1:]
    earlier = jnp.concatenate([jnp.zeros((shares.shape[0], 1), jnp.int32), bounds[:, :-1]], axis=1)
    return (1 + bounds - earlier).astype(jnp.int32)


def draw_image_lengths(key, part):
    key = jax.random.fold_in(key, 7)
    first_key, second_key, third_key = jax.random.split(key, 3)
    lowest = max(IMGS, TOK_DEV // 6)
    highest = TOK_DEV // 2
    jitter_span = max(1, TOK_DEV // 24)
    ramp = lowest + jnp.arange(N_DP, dtype=jnp.int32) * (highest - lowest) // max(1, N_DP - 1)
    jitter = jax.random.randint(first_key, (N_DP,), -jitter_span, jitter_span + 1).astype(jnp.int32)
    counts = jnp.clip(ramp + jitter, lowest, highest).astype(jnp.int32)
    fullest = jax.random.randint(second_key, (), 0, N_DP)
    shares = jax.random.randint(third_key, (N_DP, IMGS), 1, 9).astype(jnp.int32)
    drawn = split_counts(counts, shares)
    half = TOK_DEV // 2
    rest_total = jnp.full((N_DP,), TOK_DEV - half, jnp.int32)
    rest = split_counts(rest_total, shares[:, 1:])
    packed_full = jnp.concatenate([jnp.full((N_DP, 1), half, jnp.int32), rest], axis=1)
    chosen = (jnp.arange(N_DP) == fullest)[:, None]
    return jnp.where(chosen, packed_full, drawn).astype(jnp.int32)


def strengthened(result, key, source, target, parts, factor):
    owner, partner = [(jnp.arange(result.shape[position]) // (result.shape[position] // parts)).reshape([-1 if axis == position else 1 for axis in range(result.ndim)]) for position in (source, target)]
    chosen = jax.random.permutation(key, parts)[partner]
    strong = (owner == chosen) | (owner == (partner + parts // 2) % parts)
    return jnp.where(strong, factor * result, result)


def level_of(key, extent, pieces, smallest, high):
    def one(axis_at, blocks):
        heights = jax.random.uniform(jax.random.fold_in(jax.random.fold_in(key, 6), axis_at), (blocks,), jnp.float32, smallest / len(pieces), high / len(pieces))
        return jnp.repeat(jnp.exp(heights), extent[axis_at] // blocks).reshape((-1,) + (1,) * (len(extent) - axis_at - 1))

    gain = one(*pieces[0])
    for cut in pieces[1:]:
        gain = gain * one(*cut)
    return gain


def gaussian(own_key, shape, scale, most, pieces=(), held_as=jnp.bfloat16):
    drawn = jax.random.normal(own_key, shape, jnp.float32) * scale
    if len(pieces) > 0:
        drawn = level_of(own_key, shape, pieces, -0.22, 0.18) * drawn
    return jnp.clip(drawn, min=-most, max=most).astype(held_as)


def heavy_noise(own_key, shape, width, reach, pieces, heavy, kind=jnp.bfloat16):
    entries = width * jax.random.normal(own_key, shape, jnp.float32)
    if pieces:
        entries = entries * level_of(own_key, shape, pieces, -0.22, 0.18)
    return jnp.clip(strengthened(entries, jax.random.fold_in(own_key, 3), *heavy), -reach, reach).astype(kind)


def setup_inputs(seed: int = 0) -> dict:
    arg_keys = jax.random.split(jax.random.key(seed), 8)
    queries = draw_queries(jax.random.fold_in(arg_keys[7], 71), 0)
    keys = draw_keys(jax.random.fold_in(arg_keys[7], 71), 0)
    values = gaussian(arg_keys[2], (TOKENS, HL), 1.0, 6.0, ((0, 32), (1, 8)))
    upstream = heavy_noise(arg_keys[3], (TOKENS, D), 1.0, 6.0, ((0, 32), (1, 8)), (0, 1, 32, 2.75))
    out_weight = gaussian(arg_keys[4], (D, HL), HL ** -0.5, 0.109375, ((0, 32), (1, 8)))
    fisher = jnp.clip(jnp.exp(math.log(0.2) - 2.3025851 * jax.random.uniform(arg_keys[5], (D, HL), jnp.float32) ** level_of(arg_keys[5], (D, HL), ((0, 32), (1, 8)), -0.2, 0.2)), 0.02, 0.2)
    image_lengths = draw_image_lengths(jax.random.fold_in(arg_keys[7], 71), 0)
    return {"queries": queries, "keys": keys, "values": values, "upstream": upstream, "out_weight": out_weight, "fisher": fisher, "image_lengths": image_lengths}


FLOOR_SCORE = -1.0e30


def segment_layout(lengths, slot_count):
    finish = jnp.cumsum(lengths).astype(jnp.int32)
    positions = jnp.arange(slot_count, dtype=jnp.int32)
    segment = jnp.sum((positions[:, None] >= finish[None, :]).astype(jnp.int32), axis=1)
    inside = positions < finish[-1]
    return segment, inside


def head_backward(query_head, key_head, value_head, grad_head, allowed):
    score_scale = HD ** -0.5
    scores = jnp.dot(query_head, key_head.T, preferred_element_type=jnp.float32) * score_scale
    shifted = jnp.where(allowed, scores, FLOOR_SCORE)
    largest = jnp.max(shifted, axis=1, keepdims=True)
    weights = jnp.where(allowed, jnp.exp(shifted - largest), 0.0)
    summed = jnp.sum(weights, axis=1, keepdims=True)
    probs = weights / summed
    probs_low = probs.astype(jnp.bfloat16)
    attended = jnp.dot(probs_low, value_head, preferred_element_type=jnp.float32).astype(jnp.bfloat16)
    diagonal_term = jnp.sum(grad_head.astype(jnp.float32) * attended.astype(jnp.float32), axis=1, keepdims=True)
    grad_probs = jnp.dot(grad_head, value_head.T, preferred_element_type=jnp.float32)
    grad_scores = (probs * (grad_probs - diagonal_term)).astype(jnp.bfloat16)
    grad_query = (jnp.dot(grad_scores, key_head, preferred_element_type=jnp.float32) * score_scale).astype(jnp.bfloat16)
    grad_key = (jnp.dot(grad_scores.T, query_head, preferred_element_type=jnp.float32) * score_scale).astype(jnp.bfloat16)
    grad_value = jnp.dot(probs_low.T, grad_head, preferred_element_type=jnp.float32).astype(jnp.bfloat16)
    return attended, grad_query, grad_key, grad_value


def reference(queries, keys, values, upstream, out_weight, fisher, image_lengths):
    def split_heads(array):
        return array.reshape(TOK_DEV, H, HD).transpose(1, 0, 2)

    def join_heads(array):
        return array.transpose(1, 0, 2).reshape(TOK_DEV, H * HD)

    def one_sequence(packed):
        query_rows, key_rows, value_rows, grad_rows, lengths = packed
        segment, inside = segment_layout(lengths, TOK_DEV)
        grad_masked = jnp.where(inside[:, None], grad_rows, jnp.zeros_like(grad_rows))
        grad_attn = jnp.dot(grad_masked, out_weight, preferred_element_type=jnp.float32).astype(jnp.bfloat16)
        allowed = segment[:, None] == segment[None, :]

        def one_head(group):
            return head_backward(group[0], group[1], group[2], group[3], allowed)

        results = lax.map(one_head, (split_heads(query_rows), split_heads(key_rows), split_heads(value_rows), split_heads(grad_attn)))
        return (join_heads(results[0]), join_heads(results[1]), join_heads(results[2]), join_heads(results[3]), grad_masked)

    def by_sequence(array):
        return array.reshape(N_DP, TOK_DEV, array.shape[1])

    attended, grad_queries, grad_keys, grad_values, grad_masked = lax.map(
        one_sequence, (by_sequence(queries), by_sequence(keys), by_sequence(values), by_sequence(upstream), image_lengths))
    weight_grad = jnp.dot(grad_masked.reshape(TOKENS, D).T, attended.reshape(TOKENS, H * HD), preferred_element_type=jnp.float32)
    patch_total = jnp.sum(image_lengths).astype(jnp.float32)
    fisher_next = fisher + weight_grad * weight_grad / patch_total
    return (grad_queries.reshape(TOKENS, H * HD), grad_keys.reshape(TOKENS, H * HD), grad_values.reshape(TOKENS, H * HD), weight_grad, fisher_next)
```

```python
import functools

import jax
import jax.numpy as jnp
from jax import lax
from jax.experimental import pallas as pl
from jax.experimental.pallas import tpu as pltpu
from jax.sharding import PartitionSpec as P

MESH = pl.DeviceIdType.MESH
HD = 128
NX, NY, NZ = 4, 4, 8
FLOOR_SCORE = -1e30
F32, BF16 = jnp.float32, jnp.bfloat16
N_REMOTE = 96
N_LOCAL = 16

NN = (((1,), (0,)), ((), ()))
NT = (((1,), (1,)), ((), ()))
TN = (((0,), (0,)), ((), ()))


def dot(a, b, dims):
    return lax.dot_general(a, b, dims, preferred_element_type=F32)


def kernel(
    len_ref, q_hbm, k_hbm, v_hbm, up_hbm, w_hbm, fisher_hbm,
    gq_hbm, gk_hbm, gv_hbm, wg_hbm, fn_hbm,
    q_v, k_v, v_v, up_v, fisher_v, gq_v, gk_v, gv_v, wg_v, fn_v,
    up_t, g_all, g_relay, w_all, w_t, att_t, probs_t,
    xs_far, xr_far, xs_sum, xr_sum, x_acc, grad_t,
    zs, zr, z_acc, cnt, cnt_x, cnt_z,
    send_sem, recv_sem, local_sem,
):
    tokens = up_v.shape[0]
    rows = w_hbm.shape[0]
    half = rows // 2
    width = q_v.shape[1]
    heads = width // HD
    scale = HD ** (-0.5)

    dp, tau = lax.axis_index("dp"), lax.axis_index("tensor")
    z, x = dp // NX, dp % NX
    y, c = tau // 2, tau % 2

    def at(dz=0, dx=0, dy=0, other=False):
        pz, px, py = (z + dz + NZ) % NZ, (x + dx + NX) % NX, (y + dy + NY) % NY
        return (pz * NX + px, py * 2 + (1 - c if other else c))

    def block(index, start=0, size=rows):
        return pl.ds(pl.multiple_of(index * rows + start, 16), size)

    sent = []
    index_of = {}

    def message(name, src, dst, to):
        number = index_of.setdefault(name, len(index_of))
        return pltpu.make_async_remote_copy(
            src_ref=src, dst_ref=dst, send_sem=send_sem.at[number], recv_sem=recv_sem.at[number],
            device_id=to, device_id_type=MESH,
        )

    pending = {}

    def send(name, src, dst, to):
        copy = message(name, src, dst, to)
        copy.start()
        pending[name] = copy
        sent.append(copy)

    def arrive(name):
        pending[name].wait_recv()

    locals_ = {}

    def load(name, src, dst):
        copy = pltpu.make_async_copy(src, dst, local_sem.at[len(locals_)])
        copy.start()
        locals_[name] = copy

    load("up", up_hbm, up_v)
    load("q", q_hbm, q_v)
    load("k", k_hbm, k_v)
    load("v", v_hbm, v_v)
    load("w", w_hbm, w_all.at[block(z)])
    load("fisher", fisher_hbm, fisher_v)

    peers = [at(dz=d) for d in range(1, NZ)] + [at(dx=d) for d in range(1, NX)]
    peers += [at(dy=1), at(dy=-1), at(other=True)]
    barrier = pltpu.get_barrier_semaphore()
    for peer in peers:
        pl.semaphore_signal(barrier, inc=1, device_id=peer, device_id_type=MESH)

    finish = []
    total = jnp.int32(0)
    for j in range(len_ref.shape[1]):
        total = total + len_ref[0, j]
        finish.append(total)
    filled = finish[-1]
    cnt[...] = jnp.full(cnt.shape, filled.astype(F32), F32)

    locals_["up"].wait()
    with jax.named_scope("transpose_upstream"):
        inside = lax.broadcasted_iota(jnp.int32, (tokens, HD), 0) < filled
        for j in range(up_v.shape[1] // HD):
            piece = up_v[:, j * HD:(j + 1) * HD].astype(F32)
            up_t[j * HD:(j + 1) * HD, :] = jnp.where(inside, piece, 0.0).T.astype(BF16)
        g_all[0, block(tau), :] = up_t[block(x), :]

    with jax.named_scope("entry_barrier"):
        pl.semaphore_wait(barrier, len(peers))

    A, B = pl.ds(0, half), pl.ds(half, half)

    def w_rows(index, part):
        return w_all.at[block(index, 0 if part == "A" else half, half)]

    for part, cut in (("A", A), ("B", B)):
        send(f"w+1{part}", w_hbm.at[cut], w_rows(z, part), at(dz=1))
    for part, cut in (("B", B), ("A", A)):
        send(f"w-1{part}", w_hbm.at[cut], w_rows(z, part), at(dz=-1))
    x_next, x_prev, x_far = (x + 1) % NX, (x + NX - 1) % NX, (x + 2) % NX
    send("g2A", up_t.at[block(x_far, 0, half)], g_relay.at[0], at(dx=1))
    send("g2B", up_t.at[block(x_far, half, half)], g_relay.at[1], at(dx=-1))
    send("g1+", up_t.at[block(x_next)], g_all.at[3, block(tau)], at(dx=1))
    send("g1-", up_t.at[block(x_prev)], g_all.at[1, block(tau)], at(dx=-1))
    for d in range(1, NX):
        send(f"cx{d}", cnt, cnt_x.at[d], at(dx=d))

    def spread(slot):
        piece = g_all.at[slot, block(tau)]
        send(f"y{slot}+", piece, piece, at(dy=1))
        send(f"y{slot}-", piece, piece, at(dy=-1))
        send(f"s{slot}0", piece, piece, at(other=True))

    def y_rows(dy, part=None):
        row = ((y + dy + NY) % NY) * 2 + c
        if part is None:
            return block(row)
        return block(row, 0 if part == "A" else half, half)

    def relay_y(slot):
        arrive(f"y{slot}+")
        piece = g_all.at[slot, y_rows(-1, "A")]
        send(f"y{slot}A", piece, piece, at(dy=1))
        piece = g_all.at[slot, y_rows(-1)]
        send(f"s{slot}1", piece, piece, at(other=True))
        arrive(f"y{slot}-")
        piece = g_all.at[slot, y_rows(1, "B")]
        send(f"y{slot}B", piece, piece, at(dy=-1))
        piece = g_all.at[slot, y_rows(1)]
        send(f"s{slot}2", piece, piece, at(other=True))

    def end_y(slot):
        arrive(f"y{slot}A")
        arrive(f"y{slot}B")
        piece = g_all.at[slot, y_rows(2)]
        send(f"s{slot}3", piece, piece, at(other=True))

    def end_core(slot):
        for j in range(4):
            arrive(f"s{slot}{j}")

    def relay_w(step, part, directions="+-"):
        for sign in directions:
            arrive(f"w{sign}{step - 1}{part}")
            one = 1 if sign == "+" else -1
            source = (z - one * (step - 1) + NZ) % NZ
            send(f"w{sign}{step}{part}", w_rows(source, part), w_rows(source, part), at(dz=one))

    spread(0)

    u_position = lax.broadcasted_iota(jnp.int32, (tokens, 1), 0)
    t_position = lax.broadcasted_iota(jnp.int32, (1, tokens), 1)
    u_segment = jnp.zeros((tokens, 1), jnp.int32)
    t_segment = jnp.zeros((1, tokens), jnp.int32)
    for end in finish:
        u_segment += (u_position >= end).astype(jnp.int32)
        t_segment += (t_position >= end).astype(jnp.int32)

    def forward(h):
        span = pl.ds(h * HD, HD)
        scores = dot(k_v[:, span], q_v[:, span], NT) * scale
        shifted = jnp.where(u_segment == t_segment, scores, FLOOR_SCORE)
        largest = jnp.max(shifted, axis=0, keepdims=True)
        weights = jnp.exp(shifted - largest)
        probs = weights * (1.0 / jnp.sum(weights, axis=0, keepdims=True))
        probs_t[h] = probs
        att_t[0, span, :] = dot(v_v[:, span], probs.astype(BF16), TN).astype(BF16)

    for name in ("q", "k", "v"):
        locals_[name].wait()
    with jax.named_scope("forward0"):
        forward(0)
    with jax.named_scope("relay_g"):
        arrive("g2A")
        send("g2a", g_relay.at[0], g_all.at[2, block(tau, 0, half)], at(dx=1))
        arrive("g2B")
        send("g2b", g_relay.at[1], g_all.at[2, block(tau, half, half)], at(dx=-1))
    with jax.named_scope("forward1"):
        forward(1)
    with jax.named_scope("relay_w2A"):
        relay_w(2, "A", "+")
        relay_w(2, "B", "-")
    with jax.named_scope("forward2"):
        forward(2)
    send("a+", att_t.at[0], att_t.at[3], at(dx=1))
    send("a-", att_t.at[0], att_t.at[1], at(dx=-1))

    with jax.named_scope("relay_w2B"):
        relay_w(2, "B", "+")
        relay_w(2, "A", "-")
    with jax.named_scope("relay_y0"):
        relay_y(0)
    with jax.named_scope("spread2"):
        arrive("g2a")
        arrive("g2b")
        spread(2)
    with jax.named_scope("spread13"):
        arrive("g1+")
        spread(3)
        arrive("g1-")
        spread(1)
    with jax.named_scope("counts"):
        for d in range(1, NX):
            arrive(f"cx{d}")
        cnt_z[0] = cnt[...] + cnt_x[1] + cnt_x[2] + cnt_x[3]
        for d in range(1, NZ):
            send(f"cz{d}", cnt_z.at[0], cnt_z.at[d], at(dz=d))
    with jax.named_scope("relay_w3A"):
        relay_w(3, "A", "+")
        relay_w(3, "B", "-")
    with jax.named_scope("relay_w3B"):
        relay_w(3, "B", "+")
        relay_w(3, "A", "-")
    with jax.named_scope("relay_a"):
        arrive("a+")
        send("aA", att_t.at[3, pl.ds(0, width // 2)], att_t.at[2, pl.ds(0, width // 2)], at(dx=1))
        arrive("a-")
        send("aB", att_t.at[1, pl.ds(width // 2, width // 2)], att_t.at[2, pl.ds(width // 2, width // 2)], at(dx=-1))
    with jax.named_scope("relay_w4"):
        relay_w(4, "A", "+")
        relay_w(4, "B", "-")
    with jax.named_scope("relay_y2"):
        end_y(0)
        relay_y(2)
    with jax.named_scope("relay_y13"):
        relay_y(3)
        relay_y(1)
        end_y(2)
    with jax.named_scope("end_w"):
        arrive("w+3B")
        arrive("w-3A")
        arrive("w+4A")
        arrive("w-4B")
        locals_["w"].wait()
        for j in range(w_all.shape[0] // HD):
            w_t[:, j * HD:(j + 1) * HD] = w_all[j * HD:(j + 1) * HD, :].T

    def grad_part(slot):
        return dot(w_t[...], g_all[slot], NN)

    def weight_part(offset, slot):
        target = (z + offset + NZ) % NZ
        for j in range(NX):
            term = dot(g_all[j, block(target), :], att_t[j], NT)
            if j == 0:
                z_acc[slot] = term
            else:
                z_acc[slot] += term

    x_half = width // 2
    XA, XB = pl.ds(0, x_half), pl.ds(x_half, x_half)
    with jax.named_scope("part_x_far"):
        end_core(2)
        xs_far[...] = grad_part(2).astype(BF16)
        send("rA", xs_far.at[XA], xr_far.at[0], at(dx=1))
        send("rB", xs_far.at[XB], xr_far.at[1], at(dx=-1))
    with jax.named_scope("end_y13"):
        end_y(3)
        end_y(1)
        end_core(0)
        end_core(3)
        x_acc[1] = grad_part(3)
        end_core(1)
        x_acc[0] = grad_part(1)
    with jax.named_scope("end_a"):
        arrive("aA")
        arrive("aB")

    halves = {"A": A, "B": B}
    slot_of = {}

    def send_z(sign, step, part, slot):
        cut = halves[part]
        value = z_acc[slot, cut, :]
        before = (sign, step - 1, part)
        if before in slot_of:
            arrive(f"z{sign}{step - 1}{part}")
            value = value + zr[slot_of[before]].astype(F32)
        mine = slot_of.setdefault((sign, step, part), len(slot_of))
        zs[mine] = value.astype(BF16)
        send(f"z{sign}{step}{part}", zs.at[mine], zr.at[mine], at(dz=1 if sign == "+" else -1))

    with jax.named_scope("part_z4"):
        weight_part(4, 0)
        send_z("+", 1, "A", 0)
        send_z("-", 1, "B", 0)
    with jax.named_scope("sum_x1"):
        arrive("rA")
        x_acc[0, XA, :] += xr_far[0].astype(F32)
        xs_sum[0] = x_acc[0].astype(BF16)
        send("r+", xs_sum.at[0], xr_sum.at[0], at(dx=1))
        arrive("rB")
        x_acc[1, XB, :] += xr_far[1].astype(F32)
        xs_sum[1] = x_acc[1].astype(BF16)
        send("r-", xs_sum.at[1], xr_sum.at[1], at(dx=-1))
    with jax.named_scope("part_z3"):
        weight_part(3, 0)
        send_z("+", 2, "B", 0)
        weight_part(-3, 1)
        send_z("-", 2, "A", 1)
        send_z("+", 2, "A", 0)
        send_z("-", 2, "B", 1)
    with jax.named_scope("part_z2"):
        weight_part(2, 0)
        weight_part(-2, 1)
        send_z("+", 3, "B", 0)
        send_z("-", 3, "A", 1)
        send_z("+", 3, "A", 0)
        send_z("-", 3, "B", 1)
    with jax.named_scope("part_x0"):
        x_acc[0] = grad_part(0)
    with jax.named_scope("part_z1"):
        weight_part(1, 0)
        weight_part(-1, 1)
        send_z("+", 4, "B", 0)
        send_z("-", 4, "A", 1)
        send_z("+", 4, "A", 0)
        send_z("-", 4, "B", 1)
    with jax.named_scope("end_x"):
        arrive("r+")
        arrive("r-")
        grad_t[...] = (x_acc[0] + xr_sum[0].astype(F32) + xr_sum[1].astype(F32)).astype(BF16)

    def backward(h):
        span = pl.ds(h * HD, HD)
        probs = probs_t[h]
        out_grad = grad_t[span, :]
        diagonal = jnp.sum(out_grad.astype(F32) * att_t[0, span, :].astype(F32), axis=0, keepdims=True)
        grad_probs = dot(v_v[:, span], out_grad, NN)
        grad_scores = (probs * (grad_probs - diagonal)).astype(BF16)
        gk_v[:, span] = (dot(grad_scores, q_v[:, span], NN) * scale).astype(BF16)
        gq_v[:, span] = (dot(grad_scores, k_v[:, span], TN) * scale).astype(BF16)
        gv_v[:, span] = dot(probs.astype(BF16), out_grad, NT).astype(BF16)

    with jax.named_scope("backward"):
        for h in range(heads):
            backward(h)
    load("gq", gq_v, gq_hbm)
    load("gk", gk_v, gk_hbm)
    load("gv", gv_v, gv_hbm)

    with jax.named_scope("part_z0"):
        weight_part(0, 0)
        for d in range(1, NZ):
            arrive(f"cz{d}")
        patches = cnt_z[0]
        for d in range(1, NZ):
            patches = patches + cnt_z[d]
        inverse = 1.0 / patches[0:1, 0:1]
        locals_["fisher"].wait()
    with jax.named_scope("end_z"):
        for part in ("B", "A"):
            cut = halves[part]
            value = z_acc[0, cut, :]
            for sign in "+-":
                arrive(f"z{sign}4{part}")
                value = value + zr[slot_of[(sign, 4, part)]].astype(F32)
            wg_v[cut, :] = value
            fn_v[cut, :] = fisher_v[cut, :] + value * value * inverse
    load("wg", wg_v, wg_hbm)
    load("fn", fn_v, fn_hbm)

    with jax.named_scope("drain"):
        for copy in sent:
            copy.wait_send()
        for name in ("gq", "gk", "gv", "wg", "fn"):
            locals_[name].wait()


def per_device(queries, keys, values, upstream, out_weight, fisher, image_lengths):
    tokens, width = queries.shape
    rows = out_weight.shape[0]
    half = rows // 2
    heads = width // HD
    hbm = pl.BlockSpec(memory_space=pl.ANY)
    vm = pltpu.VMEM
    scratch = [
        vm((tokens, width), BF16),
        vm((tokens, width), BF16),
        vm((tokens, width), BF16),
        vm(upstream.shape, BF16),
        vm((rows, width), F32),
        vm((tokens, width), BF16),
        vm((tokens, width), BF16),
        vm((tokens, width), BF16),
        vm((rows, width), F32),
        vm((rows, width), F32),
        vm((upstream.shape[1], tokens), BF16),
        vm((NX, NZ * rows, tokens), BF16),
        vm((2, half, tokens), BF16),
        vm((NZ * rows, width), BF16),
        vm((width, NZ * rows), BF16),
        vm((NX, width, tokens), BF16),
        vm((heads, tokens, tokens), F32),
        vm((width, tokens), BF16),
        vm((2, width // 2, tokens), BF16),
        vm((2, width, tokens), BF16),
        vm((2, width, tokens), BF16),
        vm((2, width, tokens), F32),
        vm((width, tokens), BF16),
        vm((14, half, width), BF16),
        vm((14, half, width), BF16),
        vm((2, rows, width), F32),
        vm((8, HD), F32),
        vm((NX, 8, HD), F32),
        vm((NZ, 8, HD), F32),
        pltpu.SemaphoreType.DMA((N_REMOTE,)),
        pltpu.SemaphoreType.DMA((N_REMOTE,)),
        pltpu.SemaphoreType.DMA((N_LOCAL,)),
    ]
    return pl.pallas_call(
        kernel,
        out_shape=[
            jax.ShapeDtypeStruct((tokens, width), BF16),
            jax.ShapeDtypeStruct((tokens, width), BF16),
            jax.ShapeDtypeStruct((tokens, width), BF16),
            jax.ShapeDtypeStruct((rows, width), F32),
            jax.ShapeDtypeStruct((rows, width), F32),
        ],
        in_specs=[pl.BlockSpec(memory_space=pltpu.SMEM)] + [hbm] * 6,
        out_specs=[hbm] * 5,
        scratch_shapes=scratch,
        compiler_params=pltpu.CompilerParams(
            collective_id=0, has_side_effects=True, vmem_limit_bytes=40 * 1024 * 1024
        ),
    )(image_lengths, queries, keys, values, upstream, out_weight, fisher)


def solution(mesh):
    placed = P("dp", "tensor")
    return jax.shard_map(
        per_device,
        mesh=mesh,
        in_specs=(placed,) * 6 + (P("dp", None),),
        out_specs=(placed,) * 5,
        check_vma=False,
    )
```

```python
import functools

import jax
import jax.numpy as jnp
from jax import lax
from jax.experimental import pallas as pl
from jax.experimental.pallas import tpu as pltpu
from jax.sharding import PartitionSpec as P

MESH = pl.DeviceIdType.MESH
HD = 128
NX, NY, NZ = 4, 4, 8
FLOOR_SCORE = -1e30
F32, BF16 = jnp.float32, jnp.bfloat16
N_REMOTE = 128
N_LOCAL = 16
VMEM_LIMIT = 48 * 1024 * 1024

ORDER = (
    "start", "fwd0", "fwd1", "fwd2", "at", "spread30", "ry0+0", "ry0-0", "spread10", "rw+2A", "rw-2B",
    "spread31", "ry0+1", "ry0-1", "spread11", "rw+2B", "rw-2A", "spread20", "ry3+0", "ry3-0", "spread21",
    "rw+3A", "rw-3B", "ey00", "ry1-0", "ry1+0", "ry3-1", "rw+3B", "rw-3A", "ry3+1", "ey01", "ry1+1", "ry1-1",
    "rw+4A", "rw-4B", "counts", "ry2+0", "ry2-0", "ey30", "ry2-1", "ry2+1", "ey31", "wt", "ey10", "ey11",
    "px3", "ey20", "ey21", "px1", "px2", "px0", "pz4", "sz+1A0", "sz+1A1", "sz-1B0", "sz-1B1", "pz3",
    "sz+2B0", "sz+2B1", "pz-3", "sz-2A0", "sz-2A1", "pz2", "pz-2", "pz1", "pz-1", "pz0", "sz+2A0", "sz-2B0",
    "sz+2A1", "sz-2B1", "sz+3B0", "sz-3A0", "sz+3B1", "sz-3A1", "sz+3A0", "sz-3B0", "sz+3A1", "sz-3B1",
    "sz+4B0", "sz-4A0", "sz+4B1", "sz-4A1", "sz+4A0", "sz-4B0", "sz+4A1", "sz-4B1", "bwd", "end",
)

NN = (((1,), (0,)), ((), ()))
NT = (((1,), (1,)), ((), ()))
TN = (((0,), (0,)), ((), ()))


def dot(a, b, dims):
    return lax.dot_general(a, b, dims, preferred_element_type=F32)


def kernel(
    len_hbm, q_hbm, k_hbm, v_hbm, up_hbm, w_hbm, fisher_hbm,
    gq_v, gk_v, gv_v, wg_v, fn_v,
    q_v, k_v, v_v, up_v, fisher_v,
    up_t, g_all, w_all, w_t, att_t, probs_t,
    xs, xr, x_own, grad_t,
    zs, zr, z_acc, cnt, cnt_x, cnt_z, len_ref,
    send_sem, recv_sem, local_sem,
):
    tokens = up_v.shape[0]
    rows = w_hbm.shape[0]
    half = rows // 2
    width = q_v.shape[1]
    heads = width // HD
    scale = HD ** (-0.5)

    dp, tau = lax.axis_index("dp"), lax.axis_index("tensor")
    z, x = dp // NX, dp % NX
    y, c = tau // 2, tau % 2

    def at(dz=0, dx=0, dy=0, other=False):
        pz, px, py = (z + dz + NZ) % NZ, (x + dx + NX) % NX, (y + dy + NY) % NY
        return (pz * NX + px, py * 2 + (1 - c if other else c))

    def block(index, start=0, size=rows):
        return pl.ds(pl.multiple_of(index * rows + start, 16), size)

    pending = {}

    def send(name, src, dst, to):
        number = len(pending)
        copy = pltpu.make_async_remote_copy(
            src_ref=src, dst_ref=dst, send_sem=send_sem.at[number], recv_sem=recv_sem.at[number],
            device_id=to, device_id_type=MESH,
        )
        copy.start()
        pending[name] = copy

    def arrive(*names):
        for name in names:
            pending[name].wait_recv()

    locals_ = {}

    def load(name, src, dst):
        copy = pltpu.make_async_copy(src, dst, local_sem.at[len(locals_)])
        copy.start()
        locals_[name] = copy

    load("len", len_hbm, len_ref)
    load("up", up_hbm, up_v)
    load("q", q_hbm, q_v)
    load("k", k_hbm, k_v)
    load("v", v_hbm, v_v)
    load("w", w_hbm, w_all.at[block(z)])
    load("fisher", fisher_hbm, fisher_v)

    peers = [at(dz=d) for d in range(1, NZ)] + [at(dx=d) for d in range(1, NX)]
    peers += [at(dy=1), at(dy=-1), at(other=True)]
    barrier = pltpu.get_barrier_semaphore()
    for peer in peers:
        pl.semaphore_signal(barrier, inc=1, device_id=peer, device_id_type=MESH)

    locals_["len"].wait()
    finish = []
    total = jnp.int32(0)
    for j in range(len_ref.shape[1]):
        total = total + len_ref[0, j]
        finish.append(total)
    filled = finish[-1]
    cnt[...] = jnp.full(cnt.shape, filled.astype(F32), F32)

    u_position = lax.broadcasted_iota(jnp.int32, (tokens, 1), 0)
    t_position = lax.broadcasted_iota(jnp.int32, (1, tokens), 1)
    u_segment = jnp.zeros((tokens, 1), jnp.int32)
    t_segment = jnp.zeros((1, tokens), jnp.int32)
    for end in finish:
        u_segment += (u_position >= end).astype(jnp.int32)
        t_segment += (t_position >= end).astype(jnp.int32)

    locals_["up"].wait()
    inside = lax.broadcasted_iota(jnp.int32, (tokens, HD), 0) < filled
    for j in range(up_v.shape[1] // HD):
        piece = up_v[:, j * HD:(j + 1) * HD].astype(F32)
        up_t[j * HD:(j + 1) * HD, :] = jnp.where(inside, piece, 0.0).T.astype(BF16)
    g_all[0, block(tau), :] = up_t[block(x), :]
    pl.semaphore_wait(barrier, len(peers))

    def w_rows(index, part):
        return w_all.at[block(index, 0 if part == "A" else half, half)]

    def relay_w(sign, step, part):
        arrive(f"w{sign}{step - 1}{part}")
        one = 1 if sign == "+" else -1
        rows_there = w_rows((z - one * (step - 1) + NZ) % NZ, part)
        send(f"w{sign}{step}{part}", rows_there, rows_there, at(dz=one))

    def g_rows(slot, dy, part):
        return g_all.at[slot, block(((y + dy + NY) % NY) * 2 + c, part * half, half)]

    def spread(slot, part):
        if slot:
            arrive(f"g{slot}{part}")
        piece = g_rows(slot, 0, part)
        send(f"y{slot}+{part}", piece, piece, at(dy=1))
        send(f"y{slot}-{part}", piece, piece, at(dy=-1))
        send(f"s{slot}0{part}", piece, piece, at(other=True))

    def relay_y(slot, sign, part):
        arrive(f"y{slot}{sign}{part}")
        one = 1 if sign == "+" else -1
        piece = g_rows(slot, -one, part)
        if (part == 0) == (sign == "+"):
            send(f"y{slot}{sign}{part}F", piece, piece, at(dy=one))
        send(f"s{slot}{sign}{part}", piece, piece, at(other=True))

    def end_y(slot, part):
        arrive(f"y{slot}{'+' if part == 0 else '-'}{part}F")
        piece = g_rows(slot, 2, part)
        send(f"s{slot}3{part}", piece, piece, at(other=True))

    def end_core(slot):
        for j in "0+-3":
            for part in (0, 1):
                arrive(f"s{slot}{j}{part}")

    def start():
        for part, cut in (("A", pl.ds(0, half)), ("B", pl.ds(half, half))):
            send(f"w+1{part}", w_hbm.at[cut], w_rows(z, part), at(dz=1))
        for part, cut in (("B", pl.ds(half, half)), ("A", pl.ds(0, half))):
            send(f"w-1{part}", w_hbm.at[cut], w_rows(z, part), at(dz=-1))
        for part in (0, 1):
            for slot, dx in ((3, 1), (1, -1)):
                there = (x + dx + NX) % NX
                send(f"g{slot}{part}", up_t.at[block(there, part * half, half)], g_rows(slot, 0, part), at(dx=dx))
            spread(0, part)
        for part in (0, 1):
            there = (x + 2) % NX
            send(f"g2{part}", up_t.at[block(there, part * half, half)], g_rows(2, 0, part), at(dx=2))
        for d in range(1, NX):
            send(f"cx{d}", cnt, cnt_x.at[d], at(dx=d))
        for name in ("q", "k", "v"):
            locals_[name].wait()

    def forward(h):
        span = pl.ds(h * HD, HD)
        scores = dot(k_v[:, span], q_v[:, span], NT) * scale
        shifted = jnp.where(u_segment == t_segment, scores, FLOOR_SCORE)
        largest = jnp.max(shifted, axis=0, keepdims=True)
        weights = jnp.exp(shifted - largest)
        probs = weights * (1.0 / jnp.sum(weights, axis=0, keepdims=True))
        probs_t[h] = probs
        att_t[0, span, :] = dot(v_v[:, span], probs.astype(BF16), TN).astype(BF16)

    def share_attended():
        for d in (1, 3, 2):
            send(f"a{d}", att_t.at[0], att_t.at[(NX - d) % NX], at(dx=d))

    def counts():
        arrive(*(f"cx{d}" for d in range(1, NX)))
        cnt_z[0] = cnt[...] + cnt_x[1] + cnt_x[2] + cnt_x[3]
        for d in range(1, NZ):
            send(f"cz{d}", cnt_z.at[0], cnt_z.at[d], at(dz=d))

    def end_w():
        arrive("w+3B", "w-3A", "w+4A", "w-4B")
        locals_["w"].wait()
        for j in range(w_all.shape[0] // HD):
            w_t[:, j * HD:(j + 1) * HD] = w_all[j * HD:(j + 1) * HD, :].T

    def grad_part(slot):
        end_core(slot)
        term = dot(w_t[...], g_all[slot], NN)
        if slot == 0:
            x_own[...] = term
        else:
            xs[slot] = term.astype(BF16)
            send(f"r{slot}", xs.at[slot], xr.at[slot], at(dx=slot))

    def weight_part(offset):
        if offset == 4:
            arrive("a1", "a2", "a3")
        target = (z + offset + NZ) % NZ
        z_acc[offset % NZ] = sum(dot(g_all[j, block(target), :], att_t[j], NT) for j in range(NX))

    def sum_z(sign, step, name):
        first = 1 if (sign == "+") == (name[0] == "A") else 2
        offset = 5 - step if sign == "+" else step - 5
        cut = quarter_of(name)
        value = z_acc[offset % NZ, cut, :]
        mine = slot_of(sign, step, name)
        if step > first:
            arrive(f"z{sign}{step - 1}{name}")
            value = value + zr[slot_of(sign, step - 1, name)].astype(F32)
        zs[mine] = value.astype(BF16)
        send(f"z{sign}{step}{name}", zs.at[mine], zr.at[mine], at(dz=1 if sign == "+" else -1))

    quarter = rows // 4

    def quarter_of(name):
        return pl.ds((2 * (name[0] == "B") + int(name[1])) * quarter, quarter)

    def slot_of(sign, step, name):
        return (16 * (sign == "-") + 8 * (name[0] == "B") + 4 * int(name[1])) + step - 1

    def backward():
        arrive("r1", "r2", "r3")
        value = x_own[...]
        for j in (1, 3, 2):
            value = value + xr[j].astype(F32)
        grad_t[...] = value.astype(BF16)
        for h in range(heads):
            span = pl.ds(h * HD, HD)
            probs = probs_t[h]
            out_grad = grad_t[span, :]
            diagonal = jnp.sum(out_grad.astype(F32) * att_t[0, span, :].astype(F32), axis=0, keepdims=True)
            grad_probs = dot(v_v[:, span], out_grad, NN)
            grad_scores = (probs * (grad_probs - diagonal)).astype(BF16)
            gk_v[:, span] = (dot(grad_scores, q_v[:, span], NN) * scale).astype(BF16)
            gq_v[:, span] = (dot(grad_scores, k_v[:, span], TN) * scale).astype(BF16)
            gv_v[:, span] = dot(probs.astype(BF16), out_grad, NT).astype(BF16)

    def end_z():
        arrive(*(f"cz{d}" for d in range(1, NZ)))
        patches = cnt_z[0]
        for d in range(1, NZ):
            patches = patches + cnt_z[d]
        inverse = 1.0 / patches[0:1, 0:1]
        locals_["fisher"].wait()
        for name in ("B0", "B1", "A0", "A1"):
            cut = quarter_of(name)
            value = z_acc[0, cut, :]
            for sign in "+-":
                arrive(f"z{sign}4{name}")
                value = value + zr[slot_of(sign, 4, name)].astype(F32)
            wg_v[cut, :] = value
            fn_v[cut, :] = fisher_v[cut, :] + value * value * inverse

    for task in ORDER:
        if task == "start":
            start()
        elif task[:3] == "fwd":
            forward(int(task[3]))
        elif task == "at":
            share_attended()
        elif task[:6] == "spread":
            spread(int(task[6]), int(task[7]))
        elif task[:2] == "ry":
            relay_y(int(task[2]), task[3], int(task[4]))
        elif task[:2] == "ey":
            end_y(int(task[2]), int(task[3]))
        elif task[:2] == "rw":
            relay_w(task[2], int(task[3]), task[4])
        elif task == "counts":
            counts()
        elif task == "wt":
            end_w()
        elif task[:2] == "px":
            grad_part(int(task[2]))
        elif task[:2] == "pz":
            weight_part(int(task[2:]))
        elif task[:2] == "sz":
            sum_z(task[2], int(task[3]), task[4:])
        elif task == "bwd":
            backward()
        else:
            end_z()

    for copy in pending.values():
        copy.wait_send()


def copy_kernel(*refs):
    n = len(refs) // 2
    sem = refs[-1]
    copies = [pltpu.make_async_copy(refs[i], refs[n + i], sem.at[i]) for i in range(n)]
    for copy in copies:
        copy.start()
    for copy in copies:
        copy.wait()


def per_device(queries, keys, values, upstream, out_weight, fisher, image_lengths):
    tokens, width = queries.shape
    rows = out_weight.shape[0]
    heads = width // HD
    hbm = pl.BlockSpec(memory_space=pl.ANY)
    vm = pltpu.VMEM
    scratch = [
        vm((tokens, width), BF16),
        vm((tokens, width), BF16),
        vm((tokens, width), BF16),
        vm(upstream.shape, BF16),
        vm((rows, width), F32),
        vm((upstream.shape[1], tokens), BF16),
        vm((NX, NZ * rows, tokens), BF16),
        vm((NZ * rows, width), BF16),
        vm((width, NZ * rows), BF16),
        vm((NX, width, tokens), BF16),
        vm((heads, tokens, tokens), F32),
        vm((NX, width, tokens), BF16),
        vm((NX, width, tokens), BF16),
        vm((width, tokens), F32),
        vm((width, tokens), BF16),
        vm((32, rows // 4, width), BF16),
        vm((32, rows // 4, width), BF16),
        vm((NZ, rows, width), F32),
        vm((8, HD), F32),
        vm((NX, 8, HD), F32),
        vm((NZ, 8, HD), F32),
        pltpu.SMEM(image_lengths.shape, jnp.int32),
        pltpu.SemaphoreType.DMA((N_REMOTE,)),
        pltpu.SemaphoreType.DMA((N_REMOTE,)),
        pltpu.SemaphoreType.DMA((N_LOCAL,)),
    ]
    shapes = [((tokens, width), BF16)] * 3 + [((rows, width), F32)] * 2
    inputs = (image_lengths, queries, keys, values, upstream, out_weight, fisher)
    results = pl.pallas_call(
        kernel,
        out_shape=[pltpu.VMEM(*shape) for shape in shapes],
        in_specs=[hbm] * 7,
        out_specs=[pl.BlockSpec(memory_space=pltpu.VMEM)] * 5,
        scratch_shapes=scratch,
        compiler_params=pltpu.CompilerParams(
            collective_id=0, has_side_effects=True, vmem_limit_bytes=VMEM_LIMIT
        ),
    )(*(pltpu.with_memory_space_constraint(a, pltpu.HBM) for a in inputs))
    return pl.pallas_call(
        copy_kernel,
        out_shape=[pltpu.HBM(*shape) for shape in shapes],
        in_specs=[pl.BlockSpec(memory_space=pltpu.VMEM)] * 5,
        out_specs=[hbm] * 5,
        scratch_shapes=[pltpu.SemaphoreType.DMA((5,))],
        compiler_params=pltpu.CompilerParams(vmem_limit_bytes=VMEM_LIMIT),
    )(*(pltpu.with_memory_space_constraint(a, pltpu.VMEM) for a in results))


def solution(mesh):
    placed = P("dp", "tensor")
    return jax.shard_map(
        per_device,
        mesh=mesh,
        in_specs=(placed,) * 6 + (P("dp", None),),
        out_specs=(placed,) * 5,
        check_vma=False,
    )
```

```python
import functools

import jax
import jax.numpy as jnp
from jax import lax
from jax.experimental import pallas as pl
from jax.experimental.pallas import tpu as pltpu
from jax.sharding import PartitionSpec as P

MESH = pl.DeviceIdType.MESH
HD = 128
NX, NY, NZ = 4, 4, 8
FLOOR_SCORE = -1e30
F32, BF16 = jnp.float32, jnp.bfloat16
H = 2
Q = 2
N_REMOTE = 28 + 15 * H + 14 * Q
N_LOCAL = 7
VMEM_LIMIT = 48 * 1024 * 1024

ORDER = (
    "start", "fwd0", "fwd1", "fwd2", "at", "spread30", "ry0+0", "ry0-0", "spread10", "rw+2A", "rw-2B",
    "spread31", "ry0+1", "ry0-1", "spread11", "rw+2B", "rw-2A", "spread20", "ry3+0", "ry3-0", "spread21",
    "rw+3A", "rw-3B", "ey00", "ry1-0", "ry1+0", "ry3-1", "rw+3B", "rw-3A", "ry3+1", "ey01", "ry1+1", "ry1-1",
    "rw+4A", "rw-4B", "ry2+0", "ry2-0", "ey30", "ry2-1", "ry2+1", "ey31", "c4", "ey10", "ey11", "ey20",
    "ey21", "wt", "ec3", "px3", "ec1", "px1", "enda", "ec0", "ec2", "pz4", "sz+1A0", "sz+1A1", "sz-1B0",
    "sz-1B1", "pz3", "sz+2B0", "sz+2B1", "pz-3", "sz-2A0", "sz-2A1", "px2", "pz2", "pz-2", "sz+2A0", "sz-2B0",
    "sz+2A1", "sz-2B1", "pz1", "pz-1", "cx", "px0", "sz+3B0", "sz-3A0", "sz+3B1", "sz-3A1", "sz+3A0",
    "sz-3B0", "sz+3A1", "sz-3B1", "pz0", "sz+4B0", "sz-4A0", "sz+4B1", "sz-4A1", "sz+4A0", "sz-4B0", "sz+4A1",
    "sz-4B1", "bwd", "end",
)

NN = (((1,), (0,)), ((), ()))
NT = (((1,), (1,)), ((), ()))
TN = (((0,), (0,)), ((), ()))


def dot(a, b, dims):
    return lax.dot_general(a, b, dims, preferred_element_type=F32)


def kernel(
    len_hbm, q_hbm, k_hbm, v_hbm, up_hbm, w_hbm, fisher_hbm,
    gq_v, gk_v, gv_v, wg_v, fn_v,
    q_v, k_v, v_v, up_v, fisher_v,
    up_t, g_all, w_all, att_t, probs_t,
    xs, xr, x_own, grad_t,
    zs, zr, z_acc, cnt, cnt_x, cnt_z, len_ref,
    send_sem, recv_sem, local_sem,
):
    tokens = up_v.shape[0]
    rows = w_hbm.shape[0]
    half = rows // 2
    width = q_v.shape[1]
    heads = width // HD
    scale = HD ** (-0.5)

    dp, tau = lax.axis_index("dp"), lax.axis_index("tensor")
    z, x = dp // NX, dp % NX
    y, c = tau // 2, tau % 2

    def at(dz=0, dx=0, dy=0, other=False):
        pz, px, py = (z + dz + NZ) % NZ, (x + dx + NX) % NX, (y + dy + NY) % NY
        return (pz * NX + px, py * 2 + (1 - c if other else c))

    def block(index, start=0, size=rows):
        return pl.ds(pl.multiple_of(index * rows + start, 16), size)

    pending = {}
    receivers = {}
    senders = {"w": [], "c": [], "g": [], "a": [], "r": [], "x": [], "z": []}

    def send(name, src, dst, to):
        kind = "g" if name[0] in "gys" else "x" if name[:2] == "cx" else name[0]
        shared = name[:2] if name[0] == "s" else kind if kind in "arx" else name
        senders[kind].append(name)
        copy = pltpu.make_async_remote_copy(
            src_ref=src, dst_ref=dst, send_sem=send_sem.at[list(senders).index(kind)],
            recv_sem=recv_sem.at[receivers.setdefault(shared, len(receivers))],
            device_id=to, device_id_type=MESH,
        )
        copy.start()
        pending[name] = copy

    def arrive(*names):
        for name in names:
            pending[name].wait_recv()

    def all_of(kind, ref, shared):
        return pltpu.make_async_remote_copy(
            src_ref=ref, dst_ref=ref, send_sem=send_sem.at[list(senders).index(kind)],
            recv_sem=recv_sem.at[receivers[shared]], device_id=at(other=True), device_id_type=MESH,
        )

    locals_ = {}

    def load(name, src, dst):
        copy = pltpu.make_async_copy(src, dst, local_sem.at[len(locals_)])
        copy.start()
        locals_[name] = copy

    peers = [at(dz=1), at(dz=-1), at(dx=1), at(dx=2), at(dx=3), at(dy=1), at(dy=-1), at(other=True)]
    barrier = pltpu.get_barrier_semaphore()
    for peer in peers:
        pl.semaphore_signal(barrier, inc=1, device_id=peer, device_id_type=MESH)

    load("len", len_hbm, len_ref)
    load("up", up_hbm, up_v)
    load("q", q_hbm, q_v)
    load("k", k_hbm, k_v)
    load("v", v_hbm, v_v)
    load("w", w_hbm, w_all.at[block(z)])
    load("fisher", fisher_hbm, fisher_v)

    def w_rows(index, part):
        return w_all.at[block(index, 0 if part == "A" else half, half)]

    pl.semaphore_wait(barrier, len(peers))
    for part, cut in (("A", pl.ds(0, half)), ("B", pl.ds(half, half))):
        send(f"w+1{part}", w_hbm.at[cut], w_rows(z, part), at(dz=1))
    for part, cut in (("B", pl.ds(half, half)), ("A", pl.ds(0, half))):
        send(f"w-1{part}", w_hbm.at[cut], w_rows(z, part), at(dz=-1))

    locals_["len"].wait()
    finish = []
    total = jnp.int32(0)
    for j in range(len_ref.shape[1]):
        total = total + len_ref[0, j]
        finish.append(total)
    filled = finish[-1]

    u_position = lax.broadcasted_iota(jnp.int32, (tokens, 1), 0)
    t_position = lax.broadcasted_iota(jnp.int32, (1, tokens), 1)
    u_segment = jnp.zeros((tokens, 1), jnp.int32)
    t_segment = jnp.zeros((1, tokens), jnp.int32)
    for end in finish:
        u_segment += (u_position >= end).astype(jnp.int32)
        t_segment += (t_position >= end).astype(jnp.int32)

    locals_["up"].wait()
    inside = lax.broadcasted_iota(jnp.int32, (tokens, HD), 0) < filled
    for j in range(up_v.shape[1] // HD):
        piece = up_v[:, j * HD:(j + 1) * HD].astype(F32)
        up_t[j * HD:(j + 1) * HD, :] = jnp.where(inside, piece, 0.0).T.astype(BF16)
    g_all[0, block(tau), :] = up_t[block(x), :]

    def hand_count(sign, step):
        one = 1 if sign == "+" else -1
        if step > 1:
            arrive(f"c{sign}{step - 1}")
        send(f"c{sign}{step}", cnt_z.at[one * (step - 1) % NZ], cnt_z.at[one * step % NZ], at(dz=one))

    def relay_w(sign, step, part):
        arrive(f"w{sign}{step - 1}{part}")
        one = 1 if sign == "+" else -1
        rows_there = w_rows((z - one * (step - 1) + NZ) % NZ, part)
        send(f"w{sign}{step}{part}", rows_there, rows_there, at(dz=one))
        if part == ("B" if sign == "+" else "A"):
            hand_count(sign, step)

    piece_rows = rows // H

    def g_rows(slot, dy, part):
        return g_all.at[slot, block(((y + dy + NY) % NY) * 2 + c, part * piece_rows, piece_rows)]

    def spread(slot, part):
        if slot:
            arrive(f"g{slot}{part}")
        piece = g_rows(slot, 0, part)
        send(f"y{slot}+{part}", piece, piece, at(dy=1))
        send(f"y{slot}-{part}", piece, piece, at(dy=-1))
        send(f"s{slot}0{part}", piece, piece, at(other=True))

    def relay_y(slot, sign, part):
        arrive(f"y{slot}{sign}{part}")
        one = 1 if sign == "+" else -1
        piece = g_rows(slot, -one, part)
        if (part < H // 2) == (sign == "+"):
            send(f"y{slot}{sign}{part}F", piece, piece, at(dy=one))
        send(f"s{slot}{sign}{part}", piece, piece, at(other=True))

    def end_y(slot, part):
        arrive(f"y{slot}{'+' if part < H // 2 else '-'}{part}F")
        piece = g_rows(slot, 2, part)
        send(f"s{slot}3{part}", piece, piece, at(other=True))

    def end_core(slot):
        all_of("g", g_all.at[slot, pl.ds(0, 4 * rows)], f"s{slot}").wait_recv()

    def start():
        for part in range(H):
            for slot, dx in ((3, 1), (1, -1)):
                there = block((x + dx + NX) % NX, part * piece_rows, piece_rows)
                send(f"g{slot}{part}", up_t.at[there], g_rows(slot, 0, part), at(dx=dx))
            spread(0, part)
        for part in range(H):
            there = block((x + 2) % NX, part * piece_rows, piece_rows)
            send(f"g2{part}", up_t.at[there], g_rows(2, 0, part), at(dx=2))
        cnt_z[0] = jnp.full(cnt.shape, filled.astype(F32), F32)
        hand_count("+", 1)
        hand_count("-", 1)
        for name in ("q", "k", "v"):
            locals_[name].wait()

    def forward(h):
        span = pl.ds(h * HD, HD)
        scores = dot(k_v[:, span], q_v[:, span], NT) * scale
        shifted = jnp.where(u_segment == t_segment, scores, FLOOR_SCORE)
        largest = jnp.max(shifted, axis=0, keepdims=True)
        weights = jnp.exp(shifted - largest)
        probs = weights * (1.0 / jnp.sum(weights, axis=0, keepdims=True))
        probs_t[h] = probs
        att_t[0, span, :] = dot(v_v[:, span], probs.astype(BF16), TN).astype(BF16)

    def share_attended():
        for d in (1, 3, 2):
            send(f"a{d}", att_t.at[0], att_t.at[(NX - d) % NX], at(dx=d))

    def end_w():
        arrive("w+3B", "w-3A", "w+4A", "w-4B")
        locals_["w"].wait()

    def counts():
        arrive("c+4", "c-3")
        cnt[...] = sum(cnt_z[d] for d in range(NZ))
        for d in range(1, NX):
            send(f"cx{d}", cnt, cnt_x.at[d], at(dx=d))

    def grad_part(slot):
        term = dot(w_all[...], g_all[slot], TN)
        if slot == 0:
            x_own[...] = term
        else:
            xs[slot] = term.astype(BF16)
            send(f"r{slot}", xs.at[slot], xr.at[slot], at(dx=slot))

    def weight_part(offset):
        target = (z + offset + NZ) % NZ
        z_acc[offset % NZ] = sum(dot(g_all[j, block(target), :], att_t[j], NT) for j in range(NX))

    def sum_z(sign, step, name):
        first = 1 if (sign == "+") == (name[0] == "A") else 2
        offset = 5 - step if sign == "+" else step - 5
        cut = quarter_of(name)
        value = z_acc[offset % NZ, cut, :]
        mine = slot_of(sign, step, name)
        if step > first:
            arrive(f"z{sign}{step - 1}{name}")
            value = value + zr[slot_of(sign, step - 1, name)].astype(F32)
        zs[mine] = value.astype(BF16)
        send(f"z{sign}{step}{name}", zs.at[mine], zr.at[mine], at(dz=1 if sign == "+" else -1))

    quarter = rows // (2 * Q)

    def quarter_of(name):
        return pl.ds((Q * (name[0] == "B") + int(name[1])) * quarter, quarter)

    def slot_of(sign, step, name):
        return ((2 * (sign == "-") + (name[0] == "B")) * Q + int(name[1])) * 4 + step - 1

    def backward():
        all_of("r", xr.at[pl.ds(1, NX - 1)], "r").wait_recv()
        value = x_own[...]
        for j in (1, 3, 2):
            value = value + xr[j].astype(F32)
        grad_t[...] = value.astype(BF16)
        for h in range(heads):
            span = pl.ds(h * HD, HD)
            probs = probs_t[h]
            out_grad = grad_t[span, :]
            diagonal = jnp.sum(out_grad.astype(F32) * att_t[0, span, :].astype(F32), axis=0, keepdims=True)
            grad_probs = dot(v_v[:, span], out_grad, NN)
            grad_scores = (probs * (grad_probs - diagonal)).astype(BF16)
            gk_v[:, span] = (dot(grad_scores, q_v[:, span], NN) * scale).astype(BF16)
            gq_v[:, span] = (dot(grad_scores, k_v[:, span], TN) * scale).astype(BF16)
            gv_v[:, span] = dot(probs.astype(BF16), out_grad, NT).astype(BF16)

    def end_z():
        all_of("x", cnt_x.at[pl.ds(1, NX - 1)], "x").wait_recv()
        patches = cnt[...]
        for d in range(1, NX):
            patches = patches + cnt_x[d]
        inverse = 1.0 / patches[0:1, 0:1]
        locals_["fisher"].wait()
        for name in [part + str(j) for part in "BA" for j in range(Q)]:
            cut = quarter_of(name)
            value = z_acc[0, cut, :]
            for sign in "+-":
                arrive(f"z{sign}4{name}")
                value = value + zr[slot_of(sign, 4, name)].astype(F32)
            wg_v[cut, :] = value
            fn_v[cut, :] = fisher_v[cut, :] + value * value * inverse

    for task in ORDER:
        if task == "start":
            start()
        elif task[:3] == "fwd":
            forward(int(task[3]))
        elif task == "at":
            share_attended()
        elif task[:6] == "spread":
            spread(int(task[6]), int(task[7]))
        elif task[:2] == "ry":
            relay_y(int(task[2]), task[3], int(task[4]))
        elif task[:2] == "ey":
            end_y(int(task[2]), int(task[3]))
        elif task[:2] == "rw":
            relay_w(task[2], int(task[3]), task[4])
        elif task == "enda":
            all_of("a", att_t.at[pl.ds(1, NX - 1)], "a").wait_recv()
        elif task[:2] == "ec":
            end_core(int(task[2]))
        elif task == "c4":
            hand_count("+", 4)
        elif task == "cx":
            counts()
        elif task == "wt":
            end_w()
        elif task[:2] == "px":
            grad_part(int(task[2]))
        elif task[:2] == "pz":
            weight_part(int(task[2:]))
        elif task[:2] == "sz":
            sum_z(task[2], int(task[3]), task[4:])
        elif task == "bwd":
            backward()
        else:
            end_z()

    pieces = len(senders["g"]) * piece_rows // NX
    for kind, ref in (
        ("w", w_all.at[pl.ds(0, len(senders["w"]) * half)]),
        ("c", cnt_z.at[pl.ds(0, len(senders["c"]))]),
        ("g", g_all.at[:, pl.ds(0, pieces)]),
        ("a", att_t.at[pl.ds(0, NX - 1)]),
        ("r", xs.at[pl.ds(0, NX - 1)]),
        ("x", cnt_x.at[pl.ds(0, NX - 1)]),
        ("z", zs.at[pl.ds(0, len(senders["z"]))]),
    ):
        all_of(kind, ref, "a").wait_send()


def copy_kernel(*refs):
    n = len(refs) // 2
    sem = refs[-1]
    copies = [pltpu.make_async_copy(refs[i], refs[n + i], sem.at[i]) for i in range(n)]
    for copy in copies:
        copy.start()
    for copy in copies:
        copy.wait()


def per_device(queries, keys, values, upstream, out_weight, fisher, image_lengths):
    tokens, width = queries.shape
    rows = out_weight.shape[0]
    heads = width // HD
    hbm = pl.BlockSpec(memory_space=pl.ANY)
    vm = pltpu.VMEM
    scratch = [
        vm((tokens, width), BF16),
        vm((tokens, width), BF16),
        vm((tokens, width), BF16),
        vm(upstream.shape, BF16),
        vm((rows, width), F32),
        vm((upstream.shape[1], tokens), BF16),
        vm((NX, NZ * rows, tokens), BF16),
        vm((NZ * rows, width), BF16),
        vm((NX, width, tokens), BF16),
        vm((heads, tokens, tokens), F32),
        vm((NX, width, tokens), BF16),
        vm((NX, width, tokens), BF16),
        vm((width, tokens), F32),
        vm((width, tokens), BF16),
        vm((16 * Q, rows // (2 * Q), width), BF16),
        vm((16 * Q, rows // (2 * Q), width), BF16),
        vm((NZ, rows, width), F32),
        vm((8, HD), F32),
        vm((NX, 8, HD), F32),
        vm((NZ, 8, HD), F32),
        pltpu.SMEM(image_lengths.shape, jnp.int32),
        pltpu.SemaphoreType.DMA((7,)),
        pltpu.SemaphoreType.DMA((N_REMOTE,)),
        pltpu.SemaphoreType.DMA((N_LOCAL,)),
    ]
    shapes = [((tokens, width), BF16)] * 3 + [((rows, width), F32)] * 2
    inputs = (image_lengths, queries, keys, values, upstream, out_weight, fisher)
    results = pl.pallas_call(
        kernel,
        out_shape=[pltpu.VMEM(*shape) for shape in shapes],
        in_specs=[hbm] * 7,
        out_specs=[pl.BlockSpec(memory_space=pltpu.VMEM)] * 5,
        scratch_shapes=scratch,
        compiler_params=pltpu.CompilerParams(
            collective_id=0, has_side_effects=True, vmem_limit_bytes=VMEM_LIMIT
        ),
    )(*(pltpu.with_memory_space_constraint(a, pltpu.HBM) for a in inputs))
    return pl.pallas_call(
        copy_kernel,
        out_shape=[pltpu.HBM(*shape) for shape in shapes],
        in_specs=[pl.BlockSpec(memory_space=pltpu.VMEM)] * 5,
        out_specs=[hbm] * 5,
        scratch_shapes=[pltpu.SemaphoreType.DMA((5,))],
        compiler_params=pltpu.CompilerParams(vmem_limit_bytes=VMEM_LIMIT),
    )(*(pltpu.with_memory_space_constraint(a, pltpu.VMEM) for a in results))


def solution(mesh):
    placed = P("dp", "tensor")
    return jax.shard_map(
        per_device,
        mesh=mesh,
        in_specs=(placed,) * 6 + (P("dp", None),),
        out_specs=(placed,) * 5,
        check_vma=False,
    )
```

```python
import functools

import jax
import jax.numpy as jnp
from jax import lax
from jax.experimental import pallas as pl
from jax.experimental.pallas import tpu as pltpu
from jax.sharding import PartitionSpec as P

MESH = pl.DeviceIdType.MESH
HD = 128
NX, NY, NZ = 4, 4, 8
FLOOR_SCORE = -1e30
F32, BF16 = jnp.float32, jnp.bfloat16
H = 2
Q = 3
N_REMOTE = 28 + 15 * H + 14 * Q
N_LOCAL = 7
VMEM_LIMIT = 48 * 1024 * 1024

ORDER = (
    "fwd0", "fwd1", "fwd2", "at", "spread30", "ry0+0", "ry0-0", "spread10", "rw+2A", "rw-2B", "spread31",
    "ry0+1", "ry0-1", "spread11", "rw+2B", "rw-2A", "spread20", "ry3+0", "ry3-0", "spread21", "rw+3A",
    "rw-3B", "ey00", "ry1-0", "ry1+0", "ry3-1", "rw+3B", "rw-3A", "ry3+1", "ey01", "ry1+1", "ry1-1", "rw+4A",
    "rw-4B", "ry2+0", "ry2-0", "ey30", "ry2-1", "ry2+1", "ey31", "c4", "ey10", "ey11", "ey20", "ey21", "enda",
    "ec0", "ec3", "ec1", "pzp", "wt", "px3", "px1", "ec2", "pzq", "sz+1A0", "sz+1A1", "sz+1A2", "sz-1B0",
    "sz-1B1", "sz-1B2", "pz3", "sz+2B0", "sz+2B1", "sz+2B2", "pz-3", "sz-2A0", "sz-2A1", "sz-2A2", "px2",
    "pz2", "pz-2", "sz+2A0", "sz-2B0", "sz+2A1", "sz-2B1", "sz+2A2", "sz-2B2", "pz1", "pz-1", "cx", "sz+3B0",
    "sz-3A0", "sz+3B1", "sz-3A1", "sz+3B2", "sz-3A2", "sz+3A0", "sz-3B0", "sz+3A1", "sz-3B1", "sz+3A2",
    "sz-3B2", "sz+4B0", "sz-4A0", "sz+4B1", "sz-4A1", "sz+4B2", "sz-4A2", "sz+4A0", "sz-4B0", "sz+4A1",
    "sz-4B1", "sz+4A2", "sz-4B2", "px0", "pz0", "bwd", "end",
)

NN = (((1,), (0,)), ((), ()))
NT = (((1,), (1,)), ((), ()))
TN = (((0,), (0,)), ((), ()))


def dot(a, b, dims):
    return lax.dot_general(a, b, dims, preferred_element_type=F32)


def kernel(
    len_hbm, q_hbm, k_hbm, v_hbm, up_hbm, w_hbm, fisher_hbm,
    gq_v, gk_v, gv_v, wg_v, fn_v,
    q_v, k_v, v_v, up_v, fisher_v,
    up_t, g_all, w_all, att_t, probs_t,
    xs, xr, x_own, grad_t,
    zs, zr, z_acc, cnt, cnt_x, cnt_z, len_ref,
    send_sem, recv_sem, local_sem,
):
    tokens = up_v.shape[0]
    rows = w_hbm.shape[0]
    half = rows // 2
    width = q_v.shape[1]
    heads = width // HD
    scale = HD ** (-0.5)

    dp, tau = lax.axis_index("dp"), lax.axis_index("tensor")
    z, x = dp // NX, dp % NX
    y, c = tau // 2, tau % 2

    def at(dz=0, dx=0, dy=0, other=False):
        pz, px, py = (z + dz + NZ) % NZ, (x + dx + NX) % NX, (y + dy + NY) % NY
        return (pz * NX + px, py * 2 + (1 - c if other else c))

    def block(index, start=0, size=rows):
        return pl.ds(pl.multiple_of(index * rows + start, 16), size)

    pending = {}
    receivers = {}
    senders = {"w": [], "c": [], "g": [], "a": [], "r": [], "x": [], "z": []}

    def send(name, src, dst, to):
        kind = "g" if name[0] in "gys" else "x" if name[:2] == "cx" else name[0]
        shared = name[:2] if name[0] == "s" else kind if kind in "arx" else name
        senders[kind].append(name)
        copy = pltpu.make_async_remote_copy(
            src_ref=src, dst_ref=dst, send_sem=send_sem.at[list(senders).index(kind)],
            recv_sem=recv_sem.at[receivers.setdefault(shared, len(receivers))],
            device_id=to, device_id_type=MESH,
        )
        copy.start()
        pending[name] = copy

    def arrive(*names):
        for name in names:
            pending[name].wait_recv()

    def all_of(kind, ref, shared):
        return pltpu.make_async_remote_copy(
            src_ref=ref, dst_ref=ref, send_sem=send_sem.at[list(senders).index(kind)],
            recv_sem=recv_sem.at[receivers[shared]], device_id=at(other=True), device_id_type=MESH,
        )

    locals_ = {}

    def load(name, src, dst):
        copy = pltpu.make_async_copy(src, dst, local_sem.at[len(locals_)])
        copy.start()
        locals_[name] = copy

    peers = [at(dz=1), at(dz=-1), at(dx=1), at(dx=2), at(dx=3), at(dy=1), at(dy=-1), at(other=True)]
    barrier = pltpu.get_barrier_semaphore()
    for peer in peers:
        pl.semaphore_signal(barrier, inc=1, device_id=peer, device_id_type=MESH)

    load("up", up_hbm, up_v)
    load("len", len_hbm, len_ref)

    def w_rows(index, part):
        return w_all.at[block(index, 0 if part == "A" else half, half)]

    locals_["up"].wait()
    for j in range(up_v.shape[1] // HD):
        up_t[j * HD:(j + 1) * HD, :] = up_v[:, j * HD:(j + 1) * HD].T
    g_all[0, block(tau), :] = up_t[block(x), :]
    pl.semaphore_wait(barrier, len(peers))

    def hand_count(sign, step):
        one = 1 if sign == "+" else -1
        if step > 1:
            arrive(f"c{sign}{step - 1}")
        send(f"c{sign}{step}", cnt_z.at[one * (step - 1) % NZ], cnt_z.at[one * step % NZ], at(dz=one))

    def relay_w(sign, step, part):
        arrive(f"w{sign}{step - 1}{part}")
        one = 1 if sign == "+" else -1
        rows_there = w_rows((z - one * (step - 1) + NZ) % NZ, part)
        send(f"w{sign}{step}{part}", rows_there, rows_there, at(dz=one))
        if part == ("B" if sign == "+" else "A"):
            hand_count(sign, step)

    piece_rows = rows // H

    def g_rows(slot, dy, part):
        return g_all.at[slot, block(((y + dy + NY) % NY) * 2 + c, part * piece_rows, piece_rows)]

    def spread(slot, part):
        if slot:
            arrive(f"g{slot}{part}")
        piece = g_rows(slot, 0, part)
        send(f"y{slot}+{part}", piece, piece, at(dy=1))
        send(f"y{slot}-{part}", piece, piece, at(dy=-1))
        send(f"s{slot}0{part}", piece, piece, at(other=True))

    def relay_y(slot, sign, part):
        arrive(f"y{slot}{sign}{part}")
        one = 1 if sign == "+" else -1
        piece = g_rows(slot, -one, part)
        if (part < H // 2) == (sign == "+"):
            send(f"y{slot}{sign}{part}F", piece, piece, at(dy=one))
        send(f"s{slot}{sign}{part}", piece, piece, at(other=True))

    def end_y(slot, part):
        arrive(f"y{slot}{'+' if part < H // 2 else '-'}{part}F")
        piece = g_rows(slot, 2, part)
        send(f"s{slot}3{part}", piece, piece, at(other=True))

    def end_core(slot):
        all_of("g", g_all.at[slot, pl.ds(0, 4 * rows)], f"s{slot}").wait_recv()

    def start():
        for part in range(H):
            for slot, dx in ((3, 1), (1, -1)):
                there = block((x + dx + NX) % NX, part * piece_rows, piece_rows)
                send(f"g{slot}{part}", up_t.at[there], g_rows(slot, 0, part), at(dx=dx))
            spread(0, part)
        for part in range(H):
            there = block((x + 2) % NX, part * piece_rows, piece_rows)
            send(f"g2{part}", up_t.at[there], g_rows(2, 0, part), at(dx=2))
        for part, cut in (("A", pl.ds(0, half)), ("B", pl.ds(half, half))):
            send(f"w+1{part}", w_hbm.at[cut], w_rows(z, part), at(dz=1))
        for part, cut in (("B", pl.ds(half, half)), ("A", pl.ds(0, half))):
            send(f"w-1{part}", w_hbm.at[cut], w_rows(z, part), at(dz=-1))
        for name, src, dst in (
            ("q", q_hbm, q_v), ("k", k_hbm, k_v), ("v", v_hbm, v_v),
            ("w", w_hbm, w_all.at[block(z)]), ("fisher", fisher_hbm, fisher_v),
        ):
            load(name, src, dst)

    def forward(h):
        span = pl.ds(h * HD, HD)
        scores = dot(k_v[:, span], q_v[:, span], NT) * scale
        shifted = jnp.where(u_segment == t_segment, scores, FLOOR_SCORE)
        largest = jnp.max(shifted, axis=0, keepdims=True)
        weights = jnp.exp(shifted - largest)
        probs = weights * (1.0 / jnp.sum(weights, axis=0, keepdims=True))
        probs_t[h] = probs
        attended = dot(v_v[:, span], probs.astype(BF16), TN)
        att_t[0, span, :] = jnp.where(t_position < filled, attended, 0.0).astype(BF16)

    def share_attended():
        for d in (1, 3, 2):
            send(f"a{d}", att_t.at[0], att_t.at[(NX - d) % NX], at(dx=d))

    def end_w():
        arrive("w+3B", "w-3A", "w+4A", "w-4B")
        locals_["w"].wait()

    def counts():
        arrive("c+4", "c-3")
        cnt[...] = sum(cnt_z[d] for d in range(NZ))
        for d in range(1, NX):
            send(f"cx{d}", cnt, cnt_x.at[d], at(dx=d))

    def grad_part(slot):
        term = dot(w_all[...], g_all[slot], TN)
        if slot == 0:
            x_own[...] = term
        else:
            xs[slot] = term.astype(BF16)
            send(f"r{slot}", xs.at[slot], xr.at[slot], at(dx=slot))

    def weight_part(offset, slots=range(NX), more=False):
        target = (z + offset + NZ) % NZ
        term = sum(dot(g_all[j, block(target), :], att_t[j], NT) for j in slots)
        if more:
            term = z_acc[offset % NZ] + term
        z_acc[offset % NZ] = term

    def sum_z(sign, step, name):
        first = 1 if (sign == "+") == (name[0] == "A") else 2
        offset = 5 - step if sign == "+" else step - 5
        cut = quarter_of(name)
        value = z_acc[offset % NZ, cut, :]
        mine = slot_of(sign, step, name)
        if step > first:
            arrive(f"z{sign}{step - 1}{name}")
            value = value + zr[slot_of(sign, step - 1, name)].astype(F32)
        zs[mine] = value.astype(BF16)
        send(f"z{sign}{step}{name}", zs.at[mine], zr.at[mine], at(dz=1 if sign == "+" else -1))

    quarter = rows // (2 * Q)

    def quarter_of(name):
        return pl.ds((Q * (name[0] == "B") + int(name[1])) * quarter, quarter)

    def slot_of(sign, step, name):
        return ((2 * (sign == "-") + (name[0] == "B")) * Q + int(name[1])) * 4 + step - 1

    def backward():
        all_of("r", xr.at[pl.ds(1, NX - 1)], "r").wait_recv()
        value = x_own[...]
        for j in (1, 3, 2):
            value = value + xr[j].astype(F32)
        grad_t[...] = jnp.where(t_position < filled, value, 0.0).astype(BF16)
        for h in range(heads):
            span = pl.ds(h * HD, HD)
            probs = probs_t[h]
            out_grad = grad_t[span, :]
            diagonal = jnp.sum(out_grad.astype(F32) * att_t[0, span, :].astype(F32), axis=0, keepdims=True)
            grad_probs = dot(v_v[:, span], out_grad, NN)
            grad_scores = (probs * (grad_probs - diagonal)).astype(BF16)
            gk_v[:, span] = (dot(grad_scores, q_v[:, span], NN) * scale).astype(BF16)
            gq_v[:, span] = (dot(grad_scores, k_v[:, span], TN) * scale).astype(BF16)
            gv_v[:, span] = dot(probs.astype(BF16), out_grad, NT).astype(BF16)

    def end_z():
        all_of("x", cnt_x.at[pl.ds(1, NX - 1)], "x").wait_recv()
        patches = cnt[...]
        for d in range(1, NX):
            patches = patches + cnt_x[d]
        inverse = 1.0 / patches[0:1, 0:1]
        locals_["fisher"].wait()
        for name in [part + str(j) for part in "BA" for j in range(Q)]:
            cut = quarter_of(name)
            value = z_acc[0, cut, :]
            for sign in "+-":
                arrive(f"z{sign}4{name}")
                value = value + zr[slot_of(sign, 4, name)].astype(F32)
            wg_v[cut, :] = value
            fn_v[cut, :] = fisher_v[cut, :] + value * value * inverse

    start()
    locals_["len"].wait()
    finish = []
    total = jnp.int32(0)
    for j in range(len_ref.shape[1]):
        total = total + len_ref[0, j]
        finish.append(total)
    filled = finish[-1]
    u_position = lax.broadcasted_iota(jnp.int32, (tokens, 1), 0)
    t_position = lax.broadcasted_iota(jnp.int32, (1, tokens), 1)
    u_segment = jnp.zeros((tokens, 1), jnp.int32)
    t_segment = jnp.zeros((1, tokens), jnp.int32)
    for end in finish:
        u_segment += (u_position >= end).astype(jnp.int32)
        t_segment += (t_position >= end).astype(jnp.int32)
    cnt_z[0] = jnp.full(cnt.shape, filled.astype(F32), F32)
    hand_count("+", 1)
    hand_count("-", 1)
    for name in ("q", "k", "v"):
        locals_[name].wait()
    for task in ORDER:
        if task[:3] == "fwd":
            forward(int(task[3]))
        elif task == "at":
            share_attended()
        elif task[:6] == "spread":
            spread(int(task[6]), int(task[7]))
        elif task[:2] == "ry":
            relay_y(int(task[2]), task[3], int(task[4]))
        elif task[:2] == "ey":
            end_y(int(task[2]), int(task[3]))
        elif task[:2] == "rw":
            relay_w(task[2], int(task[3]), task[4])
        elif task == "enda":
            all_of("a", att_t.at[pl.ds(1, NX - 1)], "a").wait_recv()
        elif task[:2] == "ec":
            end_core(int(task[2]))
        elif task == "c4":
            hand_count("+", 4)
        elif task == "cx":
            counts()
        elif task == "wt":
            end_w()
        elif task[:2] == "px":
            grad_part(int(task[2]))
        elif task == "pzp":
            weight_part(4, (0, 1, 3))
        elif task == "pzq":
            weight_part(4, (2,), True)
        elif task[:2] == "pz":
            weight_part(int(task[2:]))
        elif task[:2] == "sz":
            sum_z(task[2], int(task[3]), task[4:])
        elif task == "bwd":
            backward()
        else:
            end_z()

    pieces = len(senders["g"]) * piece_rows // NX
    for kind, ref in (
        ("w", w_all.at[pl.ds(0, len(senders["w"]) * half)]),
        ("c", cnt_z.at[pl.ds(0, len(senders["c"]))]),
        ("g", g_all.at[:, pl.ds(0, pieces)]),
        ("a", att_t.at[pl.ds(0, NX - 1)]),
        ("r", xs.at[pl.ds(0, NX - 1)]),
        ("x", cnt_x.at[pl.ds(0, NX - 1)]),
        ("z", zs.at[pl.ds(0, len(senders["z"]))]),
    ):
        all_of(kind, ref, "a").wait_send()


def copy_kernel(*refs):
    n = len(refs) // 2
    sem = refs[-1]
    copies = [pltpu.make_async_copy(refs[i], refs[n + i], sem.at[i]) for i in range(n)]
    for copy in copies:
        copy.start()
    for copy in copies:
        copy.wait()


def per_device(queries, keys, values, upstream, out_weight, fisher, image_lengths):
    tokens, width = queries.shape
    rows = out_weight.shape[0]
    heads = width // HD
    hbm = pl.BlockSpec(memory_space=pl.ANY)
    vm = pltpu.VMEM
    scratch = [
        vm((tokens, width), BF16),
        vm((tokens, width), BF16),
        vm((tokens, width), BF16),
        vm(upstream.shape, BF16),
        vm((rows, width), F32),
        vm((upstream.shape[1], tokens), BF16),
        vm((NX, NZ * rows, tokens), BF16),
        vm((NZ * rows, width), BF16),
        vm((NX, width, tokens), BF16),
        vm((heads, tokens, tokens), F32),
        vm((NX, width, tokens), BF16),
        vm((NX, width, tokens), BF16),
        vm((width, tokens), F32),
        vm((width, tokens), BF16),
        vm((16 * Q, rows // (2 * Q), width), BF16),
        vm((16 * Q, rows // (2 * Q), width), BF16),
        vm((NZ, rows, width), F32),
        vm((8, HD), F32),
        vm((NX, 8, HD), F32),
        vm((NZ, 8, HD), F32),
        pltpu.SMEM(image_lengths.shape, jnp.int32),
        pltpu.SemaphoreType.DMA((7,)),
        pltpu.SemaphoreType.DMA((N_REMOTE,)),
        pltpu.SemaphoreType.DMA((N_LOCAL,)),
    ]
    shapes = [((tokens, width), BF16)] * 3 + [((rows, width), F32)] * 2
    inputs = (image_lengths, queries, keys, values, upstream, out_weight, fisher)
    results = pl.pallas_call(
        kernel,
        out_shape=[pltpu.VMEM(*shape) for shape in shapes],
        in_specs=[hbm] * 7,
        out_specs=[pl.BlockSpec(memory_space=pltpu.VMEM)] * 5,
        scratch_shapes=scratch,
        compiler_params=pltpu.CompilerParams(
            collective_id=0, has_side_effects=True, vmem_limit_bytes=VMEM_LIMIT
        ),
    )(*(pltpu.with_memory_space_constraint(a, pltpu.HBM) for a in inputs))
    return pl.pallas_call(
        copy_kernel,
        out_shape=[pltpu.HBM(*shape) for shape in shapes],
        in_specs=[pl.BlockSpec(memory_space=pltpu.VMEM)] * 5,
        out_specs=[hbm] * 5,
        scratch_shapes=[pltpu.SemaphoreType.DMA((5,))],
        compiler_params=pltpu.CompilerParams(vmem_limit_bytes=VMEM_LIMIT),
    )(*(pltpu.with_memory_space_constraint(a, pltpu.VMEM) for a in results))


def solution(mesh):
    placed = P("dp", "tensor")
    return jax.shard_map(
        per_device,
        mesh=mesh,
        in_specs=(placed,) * 6 + (P("dp", None),),
        out_specs=(placed,) * 5,
        check_vma=False,
    )
```

```python
import functools

import jax
import jax.numpy as jnp
from jax import lax
from jax.experimental import pallas as pl
from jax.experimental.pallas import tpu as pltpu
from jax.sharding import PartitionSpec as P

MESH = pl.DeviceIdType.MESH
HD = 128
NX, NY, NZ = 4, 4, 8
FLOOR_SCORE = -1e30
F32, BF16 = jnp.float32, jnp.bfloat16
H = 2
Q = 2
N_REMOTE = 28 + 15 * H + 14 * Q
N_LOCAL = 8
VMEM_LIMIT = 48 * 1024 * 1024

ORDER = (
    "fwd0", "fwd1", "fwd2", "at", "spread30", "ry0+0", "ry0-0", "spread10", "rw+2A", "rw-2B", "spread31",
    "ry0+1", "ry0-1", "spread11", "rw+2B", "rw-2A", "spread20", "ry3+0", "ry3-0", "spread21", "rw+3A",
    "rw-3B", "ey00", "ry1-0", "ry1+0", "ry3-1", "rw+3B", "rw-3A", "ry3+1", "ey01", "ry1+1", "ry1-1", "rw+4A",
    "rw-4B", "ry2+0", "ry2-0", "ey30", "ry2-1", "ry2+1", "ey31", "c4", "ey10", "ey11", "ey20", "ey21", "enda",
    "ec0", "ec3", "ec1", "pzp", "wt", "px3", "px1", "ec2", "pzq", "sz+1A0", "sz-1B0", "sz+1A1", "sz-1B1",
    "pz3", "pz-3", "sz+2B0", "sz-2A0", "sz+2B1", "sz-2A1", "px2", "pz2", "pz-2", "sz+2A0", "sz-2B0", "sz+2A1",
    "sz-2B1", "pz1", "pz-1", "cx", "sz+3B0", "sz-3A0", "sz+3B1", "sz-3A1", "sz+3A0", "sz-3B0", "sz+3A1",
    "sz-3B1", "sz+4B0", "sz-4A0", "sz+4B1", "sz-4A1", "sz+4A0", "sz-4B0", "sz+4A1", "sz-4B1", "px0", "pz0",
    "bwd", "end",
)

NN = (((1,), (0,)), ((), ()))
NT = (((1,), (1,)), ((), ()))
TN = (((0,), (0,)), ((), ()))


def dot(a, b, dims):
    return lax.dot_general(a, b, dims, preferred_element_type=F32)


def kernel(
    len_hbm, q_hbm, k_hbm, v_hbm, up_hbm, w_hbm, fisher_hbm,
    gq_v, gk_v, gv_v, wg_v, fn_v,
    q_v, k_v, v_v, up_v, fisher_v,
    up_t, g_all, w_all, att_t, probs_t,
    xs, xr, x_own, grad_t,
    zs, zr, z_acc, cnt, cnt_x, cnt_z, len_ref,
    send_sem, recv_sem, local_sem,
):
    tokens = up_v.shape[0]
    rows = w_hbm.shape[0]
    half = rows // 2
    width = q_v.shape[1]
    heads = width // HD
    scale = HD ** (-0.5)

    dp, tau = lax.axis_index("dp"), lax.axis_index("tensor")
    z, x = dp // NX, dp % NX
    y, c = tau // 2, tau % 2

    def at(dz=0, dx=0, dy=0, other=False):
        pz, px, py = (z + dz + NZ) % NZ, (x + dx + NX) % NX, (y + dy + NY) % NY
        return (pz * NX + px, py * 2 + (1 - c if other else c))

    def block(index, start=0, size=rows):
        return pl.ds(pl.multiple_of(index * rows + start, 16), size)

    pending = {}
    receivers = {}
    senders = {"w": [], "c": [], "g": [], "a": [], "r": [], "x": [], "z": []}

    def send(name, src, dst, to):
        kind = "g" if name[0] in "gys" else "x" if name[:2] == "cx" else name[0]
        shared = name[:2] if name[0] == "s" else kind if kind in "arx" else name
        senders[kind].append(name)
        copy = pltpu.make_async_remote_copy(
            src_ref=src, dst_ref=dst, send_sem=send_sem.at[list(senders).index(kind)],
            recv_sem=recv_sem.at[receivers.setdefault(shared, len(receivers))],
            device_id=to, device_id_type=MESH,
        )
        copy.start()
        pending[name] = copy

    def arrive(*names):
        for name in names:
            pending[name].wait_recv()

    def all_of(kind, ref, shared):
        return pltpu.make_async_remote_copy(
            src_ref=ref, dst_ref=ref, send_sem=send_sem.at[list(senders).index(kind)],
            recv_sem=recv_sem.at[receivers[shared]], device_id=at(other=True), device_id_type=MESH,
        )

    locals_ = {}

    def load(name, src, dst):
        copy = pltpu.make_async_copy(src, dst, local_sem.at[len(locals_)])
        copy.start()
        locals_[name] = copy

    peers = [at(dz=1), at(dz=-1), at(dx=1), at(dx=2), at(dx=3), at(dy=1), at(dy=-1), at(other=True)]
    barrier = pltpu.get_barrier_semaphore()
    for peer in peers:
        pl.semaphore_signal(barrier, inc=1, device_id=peer, device_id_type=MESH)

    bands = [pl.ds(j * HD, HD) for j in range(tokens // HD)]
    for j, band in enumerate(bands):
        load(f"up{j}", up_hbm.at[band], up_v.at[band])
    load("len", len_hbm, len_ref)

    def w_rows(index, part):
        return w_all.at[block(index, 0 if part == "A" else half, half)]

    for j, band in enumerate(bands):
        locals_[f"up{j}"].wait()
        up_t[:, band] = up_v[band, :].T
    g_all[0, block(tau), :] = up_t[block(x), :]
    pl.semaphore_wait(barrier, len(peers))

    def hand_count(sign, step):
        one = 1 if sign == "+" else -1
        if step > 1:
            arrive(f"c{sign}{step - 1}")
        send(f"c{sign}{step}", cnt_z.at[one * (step - 1) % NZ], cnt_z.at[one * step % NZ], at(dz=one))

    def relay_w(sign, step, part):
        arrive(f"w{sign}{step - 1}{part}")
        one = 1 if sign == "+" else -1
        rows_there = w_rows((z - one * (step - 1) + NZ) % NZ, part)
        send(f"w{sign}{step}{part}", rows_there, rows_there, at(dz=one))
        if part == ("B" if sign == "+" else "A"):
            hand_count(sign, step)

    piece_rows = rows // H

    def g_rows(slot, dy, part):
        return g_all.at[slot, block(((y + dy + NY) % NY) * 2 + c, part * piece_rows, piece_rows)]

    def spread(slot, part):
        if slot:
            arrive(f"g{slot}{part}")
        piece = g_rows(slot, 0, part)
        send(f"y{slot}+{part}", piece, piece, at(dy=1))
        send(f"y{slot}-{part}", piece, piece, at(dy=-1))
        send(f"s{slot}0{part}", piece, piece, at(other=True))

    def relay_y(slot, sign, part):
        arrive(f"y{slot}{sign}{part}")
        one = 1 if sign == "+" else -1
        piece = g_rows(slot, -one, part)
        if (part < H // 2) == (sign == "+"):
            send(f"y{slot}{sign}{part}F", piece, piece, at(dy=one))
        send(f"s{slot}{sign}{part}", piece, piece, at(other=True))

    def end_y(slot, part):
        arrive(f"y{slot}{'+' if part < H // 2 else '-'}{part}F")
        piece = g_rows(slot, 2, part)
        send(f"s{slot}3{part}", piece, piece, at(other=True))

    def end_core(slot):
        all_of("g", g_all.at[slot, pl.ds(0, 4 * rows)], f"s{slot}").wait_recv()

    def start():
        for part in range(H):
            for slot, dx in ((3, 1), (1, -1)):
                there = block((x + dx + NX) % NX, part * piece_rows, piece_rows)
                send(f"g{slot}{part}", up_t.at[there], g_rows(slot, 0, part), at(dx=dx))
            spread(0, part)
        for part in range(H):
            there = block((x + 2) % NX, part * piece_rows, piece_rows)
            send(f"g2{part}", up_t.at[there], g_rows(2, 0, part), at(dx=2))
        for part, cut in (("A", pl.ds(0, half)), ("B", pl.ds(half, half))):
            send(f"w+1{part}", w_hbm.at[cut], w_rows(z, part), at(dz=1))
        for part, cut in (("B", pl.ds(half, half)), ("A", pl.ds(0, half))):
            send(f"w-1{part}", w_hbm.at[cut], w_rows(z, part), at(dz=-1))
        for name, src, dst in (
            ("q", q_hbm, q_v), ("k", k_hbm, k_v), ("v", v_hbm, v_v),
            ("w", w_hbm, w_all.at[block(z)]), ("fisher", fisher_hbm, fisher_v),
        ):
            load(name, src, dst)

    def forward(h):
        span = pl.ds(h * HD, HD)
        scores = dot(k_v[:, span], q_v[:, span], NT) * scale
        shifted = jnp.where(u_segment == t_segment, scores, FLOOR_SCORE)
        largest = jnp.max(shifted, axis=0, keepdims=True)
        weights = jnp.exp(shifted - largest)
        probs = weights * (1.0 / jnp.sum(weights, axis=0, keepdims=True))
        probs_t[h] = probs
        attended = dot(v_v[:, span], probs.astype(BF16), TN)
        att_t[0, span, :] = jnp.where(t_position < filled, attended, 0.0).astype(BF16)

    def share_attended():
        for d in (1, 3, 2):
            send(f"a{d}", att_t.at[0], att_t.at[(NX - d) % NX], at(dx=d))

    def end_w():
        arrive("w+3B", "w-3A", "w+4A", "w-4B")
        locals_["w"].wait()

    def counts():
        arrive("c+4", "c-3")
        cnt[...] = sum(cnt_z[d] for d in range(NZ))
        for d in range(1, NX):
            send(f"cx{d}", cnt, cnt_x.at[d], at(dx=d))

    def grad_part(slot):
        term = dot(w_all[...], g_all[slot], TN)
        if slot == 0:
            x_own[...] = term
        else:
            xs[slot] = term.astype(BF16)
            send(f"r{slot}", xs.at[slot], xr.at[slot], at(dx=slot))

    def weight_part(offset, slots=range(NX), more=False):
        target = (z + offset + NZ) % NZ
        term = sum(dot(g_all[j, block(target), :], att_t[j], NT) for j in slots)
        if more:
            term = z_acc[offset % NZ] + term
        z_acc[offset % NZ] = term

    def sum_z(sign, step, name):
        first = 1 if (sign == "+") == (name[0] == "A") else 2
        offset = 5 - step if sign == "+" else step - 5
        cut = quarter_of(name)
        value = z_acc[offset % NZ, cut, :]
        mine = slot_of(sign, step, name)
        if step > first:
            arrive(f"z{sign}{step - 1}{name}")
            value = value + zr[slot_of(sign, step - 1, name)].astype(F32)
        zs[mine] = value.astype(BF16)
        send(f"z{sign}{step}{name}", zs.at[mine], zr.at[mine], at(dz=1 if sign == "+" else -1))

    quarter = rows // (2 * Q)

    def quarter_of(name):
        return pl.ds((Q * (name[0] == "B") + int(name[1])) * quarter, quarter)

    def slot_of(sign, step, name):
        return ((2 * (sign == "-") + (name[0] == "B")) * Q + int(name[1])) * 4 + step - 1

    def backward():
        all_of("r", xr.at[pl.ds(1, NX - 1)], "r").wait_recv()
        value = x_own[...]
        for j in (1, 3, 2):
            value = value + xr[j].astype(F32)
        grad_t[...] = jnp.where(t_position < filled, value, 0.0).astype(BF16)
        for h in range(heads):
            span = pl.ds(h * HD, HD)
            probs = probs_t[h]
            out_grad = grad_t[span, :]
            diagonal = jnp.sum(out_grad.astype(F32) * att_t[0, span, :].astype(F32), axis=0, keepdims=True)
            grad_probs = dot(v_v[:, span], out_grad, NN)
            grad_scores = (probs * (grad_probs - diagonal)).astype(BF16)
            gk_v[:, span] = (dot(grad_scores, q_v[:, span], NN) * scale).astype(BF16)
            gq_v[:, span] = (dot(grad_scores, k_v[:, span], TN) * scale).astype(BF16)
            gv_v[:, span] = dot(probs.astype(BF16), out_grad, NT).astype(BF16)

    def end_z():
        all_of("x", cnt_x.at[pl.ds(1, NX - 1)], "x").wait_recv()
        patches = cnt[...]
        for d in range(1, NX):
            patches = patches + cnt_x[d]
        inverse = 1.0 / patches[0:1, 0:1]
        locals_["fisher"].wait()
        for name in [part + str(j) for part in "BA" for j in range(Q)]:
            cut = quarter_of(name)
            value = z_acc[0, cut, :]
            for sign in "+-":
                arrive(f"z{sign}4{name}")
                value = value + zr[slot_of(sign, 4, name)].astype(F32)
            wg_v[cut, :] = value
            fn_v[cut, :] = fisher_v[cut, :] + value * value * inverse

    start()
    locals_["len"].wait()
    finish = []
    total = jnp.int32(0)
    for j in range(len_ref.shape[1]):
        total = total + len_ref[0, j]
        finish.append(total)
    filled = finish[-1]
    u_position = lax.broadcasted_iota(jnp.int32, (tokens, 1), 0)
    t_position = lax.broadcasted_iota(jnp.int32, (1, tokens), 1)
    u_segment = jnp.zeros((tokens, 1), jnp.int32)
    t_segment = jnp.zeros((1, tokens), jnp.int32)
    for end in finish:
        u_segment += (u_position >= end).astype(jnp.int32)
        t_segment += (t_position >= end).astype(jnp.int32)
    cnt_z[0] = jnp.full(cnt.shape, filled.astype(F32), F32)
    hand_count("+", 1)
    hand_count("-", 1)
    for name in ("q", "k", "v"):
        locals_[name].wait()
    for task in ORDER:
        if task[:3] == "fwd":
            forward(int(task[3]))
        elif task == "at":
            share_attended()
        elif task[:6] == "spread":
            spread(int(task[6]), int(task[7]))
        elif task[:2] == "ry":
            relay_y(int(task[2]), task[3], int(task[4]))
        elif task[:2] == "ey":
            end_y(int(task[2]), int(task[3]))
        elif task[:2] == "rw":
            relay_w(task[2], int(task[3]), task[4])
        elif task == "enda":
            all_of("a", att_t.at[pl.ds(1, NX - 1)], "a").wait_recv()
        elif task[:2] == "ec":
            end_core(int(task[2]))
        elif task == "c4":
            hand_count("+", 4)
        elif task == "cx":
            counts()
        elif task == "wt":
            end_w()
        elif task[:2] == "px":
            grad_part(int(task[2]))
        elif task == "pzp":
            weight_part(4, (0, 1, 3))
        elif task == "pzq":
            weight_part(4, (2,), True)
        elif task[:2] == "pz":
            weight_part(int(task[2:]))
        elif task[:2] == "sz":
            sum_z(task[2], int(task[3]), task[4:])
        elif task == "bwd":
            backward()
        else:
            end_z()

    pieces = len(senders["g"]) * piece_rows // NX
    for kind, ref in (
        ("w", w_all.at[pl.ds(0, len(senders["w"]) * half)]),
        ("c", cnt_z.at[pl.ds(0, len(senders["c"]))]),
        ("g", g_all.at[:, pl.ds(0, pieces)]),
        ("a", att_t.at[pl.ds(0, NX - 1)]),
        ("r", xs.at[pl.ds(0, NX - 1)]),
        ("x", cnt_x.at[pl.ds(0, NX - 1)]),
        ("z", zs.at[pl.ds(0, len(senders["z"]))]),
    ):
        all_of(kind, ref, "a").wait_send()


def copy_kernel(*refs):
    n = len(refs) // 2
    sem = refs[-1]
    copies = [pltpu.make_async_copy(refs[i], refs[n + i], sem.at[i]) for i in range(n)]
    for copy in copies:
        copy.start()
    for copy in copies:
        copy.wait()


def per_device(queries, keys, values, upstream, out_weight, fisher, image_lengths):
    tokens, width = queries.shape
    rows = out_weight.shape[0]
    heads = width // HD
    hbm = pl.BlockSpec(memory_space=pl.ANY)
    vm = pltpu.VMEM
    scratch = [
        vm((tokens, width), BF16),
        vm((tokens, width), BF16),
        vm((tokens, width), BF16),
        vm(upstream.shape, BF16),
        vm((rows, width), F32),
        vm((upstream.shape[1], tokens), BF16),
        vm((NX, NZ * rows, tokens), BF16),
        vm((NZ * rows, width), BF16),
        vm((NX, width, tokens), BF16),
        vm((heads, tokens, tokens), F32),
        vm((NX, width, tokens), BF16),
        vm((NX, width, tokens), BF16),
        vm((width, tokens), F32),
        vm((width, tokens), BF16),
        vm((16 * Q, rows // (2 * Q), width), BF16),
        vm((16 * Q, rows // (2 * Q), width), BF16),
        vm((NZ, rows, width), F32),
        vm((8, HD), F32),
        vm((NX, 8, HD), F32),
        vm((NZ, 8, HD), F32),
        pltpu.SMEM(image_lengths.shape, jnp.int32),
        pltpu.SemaphoreType.DMA((7,)),
        pltpu.SemaphoreType.DMA((N_REMOTE,)),
        pltpu.SemaphoreType.DMA((N_LOCAL,)),
    ]
    shapes = [((tokens, width), BF16)] * 3 + [((rows, width), F32)] * 2
    inputs = (image_lengths, queries, keys, values, upstream, out_weight, fisher)
    results = pl.pallas_call(
        kernel,
        out_shape=[pltpu.VMEM(*shape) for shape in shapes],
        in_specs=[hbm] * 7,
        out_specs=[pl.BlockSpec(memory_space=pltpu.VMEM)] * 5,
        scratch_shapes=scratch,
        compiler_params=pltpu.CompilerParams(
            collective_id=0, has_side_effects=True, vmem_limit_bytes=VMEM_LIMIT
        ),
    )(*(pltpu.with_memory_space_constraint(a, pltpu.HBM) for a in inputs))
    return pl.pallas_call(
        copy_kernel,
        out_shape=[pltpu.HBM(*shape) for shape in shapes],
        in_specs=[pl.BlockSpec(memory_space=pltpu.VMEM)] * 5,
        out_specs=[hbm] * 5,
        scratch_shapes=[pltpu.SemaphoreType.DMA((5,))],
        compiler_params=pltpu.CompilerParams(vmem_limit_bytes=VMEM_LIMIT),
    )(*(pltpu.with_memory_space_constraint(a, pltpu.VMEM) for a in results))


def solution(mesh):
    placed = P("dp", "tensor")
    return jax.shard_map(
        per_device,
        mesh=mesh,
        in_specs=(placed,) * 6 + (P("dp", None),),
        out_specs=(placed,) * 5,
        check_vma=False,
    )
```

```python
import functools

import jax
import jax.numpy as jnp
from jax import lax
from jax.experimental import pallas as pl
from jax.experimental.pallas import tpu as pltpu
from jax.sharding import PartitionSpec as P

MESH = pl.DeviceIdType.MESH
HD = 128
NX, NY, NZ = 4, 4, 8
FLOOR_SCORE = -1e30
F32, BF16 = jnp.float32, jnp.bfloat16
H = 2
Q = 2
N_REMOTE = 28 + 15 * H + 14 * Q
N_LOCAL = 8
VMEM_LIMIT = 48 * 1024 * 1024

ORDER = (
    "fwd0", "fwd1", "fwd2", "at", "spread30", "ry0+0", "ry0-0", "spread10", "rw+2A", "rw-2B", "spread31",
    "ry0+1", "ry0-1", "spread11", "rw+2B", "rw-2A", "spread20", "ry3+0", "ry3-0", "spread21", "rw+3A",
    "rw-3B", "ey00", "ry1-0", "ry1+0", "ry3-1", "rw+3B", "rw-3A", "ry3+1", "ey01", "ry1+1", "ry1-1", "rw+4A",
    "rw-4B", "ry2+0", "ry2-0", "ey30", "ry2-1", "ry2+1", "ey31", "c4", "ey10", "ey11", "ey20", "ey21", "enda",
    "ec0", "ec3", "ec1", "pzp", "wt", "px3", "px1", "ec2", "pzq", "sz+1A0", "sz-1B0", "sz+1A1", "sz-1B1",
    "pz3", "pz-3", "sz+2B0", "sz-2A0", "sz+2B1", "sz-2A1", "px2", "pz2", "pz-2", "sz+2A0", "sz-2B0", "sz+2A1",
    "sz-2B1", "pz1", "pz-1", "cx", "sz+3B0", "sz-3A0", "sz+3B1", "sz-3A1", "sz+3A0", "sz-3B0", "sz+3A1",
    "sz-3B1", "sz+4B0", "sz-4A0", "sz+4B1", "sz-4A1", "sz+4A0", "sz-4B0", "sz+4A1", "sz-4B1", "px0", "pz0",
    "bwd", "end",
)

NN = (((1,), (0,)), ((), ()))
NT = (((1,), (1,)), ((), ()))
TN = (((0,), (0,)), ((), ()))


def dot(a, b, dims):
    return lax.dot_general(a, b, dims, preferred_element_type=F32)


def kernel(
    len_hbm, q_hbm, k_hbm, v_hbm, up_hbm, w_hbm, fisher_hbm,
    gq_v, gk_v, gv_v, wg_v, fn_v,
    q_v, k_v, v_v, up_v, fisher_v,
    up_t, g_all, w_all, att_t, probs_t,
    xs, xr, x_own, grad_t,
    zs, zr, z_acc, cnt, cnt_x, cnt_z, len_ref,
    send_sem, recv_sem, local_sem,
):
    tokens = up_v.shape[0]
    rows = w_hbm.shape[0]
    half = rows // 2
    width = q_v.shape[1]
    heads = width // HD
    scale = HD ** (-0.5)

    dp, tau = lax.axis_index("dp"), lax.axis_index("tensor")
    z, x = dp // NX, dp % NX
    y, c = tau // 2, tau % 2

    def at(dz=0, dx=0, dy=0, other=False):
        pz, px, py = (z + dz + NZ) % NZ, (x + dx + NX) % NX, (y + dy + NY) % NY
        return (pz * NX + px, py * 2 + (1 - c if other else c))

    def block(index, start=0, size=rows):
        return pl.ds(pl.multiple_of(index * rows + start, 16), size)

    pending = {}
    receivers = {}
    senders = {"w": [], "c": [], "g": [], "a": [], "r": [], "x": [], "z": []}

    def send(name, src, dst, to):
        kind = "g" if name[0] in "gys" else "x" if name[:2] == "cx" else name[0]
        shared = name[:2] if name[0] == "s" else kind if kind in "arx" else name
        senders[kind].append(name)
        copy = pltpu.make_async_remote_copy(
            src_ref=src, dst_ref=dst, send_sem=send_sem.at[list(senders).index(kind)],
            recv_sem=recv_sem.at[receivers.setdefault(shared, len(receivers))],
            device_id=to, device_id_type=MESH,
        )
        copy.start()
        pending[name] = copy

    def arrive(*names):
        for name in names:
            pending[name].wait_recv()

    def all_of(kind, ref, shared):
        return pltpu.make_async_remote_copy(
            src_ref=ref, dst_ref=ref, send_sem=send_sem.at[list(senders).index(kind)],
            recv_sem=recv_sem.at[receivers[shared]], device_id=at(other=True), device_id_type=MESH,
        )

    locals_ = {}

    def load(name, src, dst):
        copy = pltpu.make_async_copy(src, dst, local_sem.at[len(locals_)])
        copy.start()
        locals_[name] = copy

    peers = [at(dz=1), at(dz=-1), at(dx=1), at(dx=2), at(dx=3), at(dy=1), at(dy=-1), at(other=True)]
    barrier = pltpu.get_barrier_semaphore()
    for peer in peers:
        pl.semaphore_signal(barrier, inc=1, device_id=peer, device_id_type=MESH)

    bands = [pl.ds(j * HD, HD) for j in range(tokens // HD)]
    for j, band in enumerate(bands):
        load(f"up{j}", up_hbm.at[band], up_v.at[band])
    load("len", len_hbm, len_ref)

    def w_rows(index, part):
        return w_all.at[block(index, 0 if part == "A" else half, half)]

    for j, band in enumerate(bands):
        locals_[f"up{j}"].wait()
        up_t[:, band] = up_v[band, :].T
    g_all[0, block(tau), :] = up_t[block(x), :]
    pl.semaphore_wait(barrier, len(peers))

    def hand_count(sign, step):
        one = 1 if sign == "+" else -1
        if step > 1:
            arrive(f"c{sign}{step - 1}")
        send(f"c{sign}{step}", cnt_z.at[one * (step - 1) % NZ], cnt_z.at[one * step % NZ], at(dz=one))

    def relay_w(sign, step, part):
        arrive(f"w{sign}{step - 1}{part}")
        one = 1 if sign == "+" else -1
        rows_there = w_rows((z - one * (step - 1) + NZ) % NZ, part)
        send(f"w{sign}{step}{part}", rows_there, rows_there, at(dz=one))
        if part == ("B" if sign == "+" else "A"):
            hand_count(sign, step)

    piece_rows = rows // H

    def g_rows(slot, dy, part):
        return g_all.at[slot, block(((y + dy + NY) % NY) * 2 + c, part * piece_rows, piece_rows)]

    def spread(slot, part):
        if slot:
            arrive(f"g{slot}{part}")
        piece = g_rows(slot, 0, part)
        send(f"y{slot}+{part}", piece, piece, at(dy=1))
        send(f"y{slot}-{part}", piece, piece, at(dy=-1))
        to_other(slot, 0, "0", part)

    def to_other(slot, dy, name, part):
        if part == H - 1:
            whole = g_all.at[slot, block(((y + dy + NY) % NY) * 2 + c)]
            send(f"s{slot}{name}", whole, whole, at(other=True))

    def relay_y(slot, sign, part):
        arrive(f"y{slot}{sign}{part}")
        one = 1 if sign == "+" else -1
        piece = g_rows(slot, -one, part)
        if (part < H // 2) == (sign == "+"):
            send(f"y{slot}{sign}{part}F", piece, piece, at(dy=one))
        to_other(slot, -one, sign, part)

    def end_y(slot, part):
        arrive(f"y{slot}{'+' if part < H // 2 else '-'}{part}F")
        to_other(slot, 2, "3", part)

    def end_core(slot):
        all_of("g", g_all.at[slot, pl.ds(0, 4 * rows)], f"s{slot}").wait_recv()

    def start():
        for part in range(H):
            for slot, dx in ((3, 1), (1, -1)):
                there = block((x + dx + NX) % NX, part * piece_rows, piece_rows)
                send(f"g{slot}{part}", up_t.at[there], g_rows(slot, 0, part), at(dx=dx))
            spread(0, part)
        for part in range(H):
            there = block((x + 2) % NX, part * piece_rows, piece_rows)
            send(f"g2{part}", up_t.at[there], g_rows(2, 0, part), at(dx=2))
        for part, cut in (("A", pl.ds(0, half)), ("B", pl.ds(half, half))):
            send(f"w+1{part}", w_hbm.at[cut], w_rows(z, part), at(dz=1))
        for part, cut in (("B", pl.ds(half, half)), ("A", pl.ds(0, half))):
            send(f"w-1{part}", w_hbm.at[cut], w_rows(z, part), at(dz=-1))
        for name, src, dst in (
            ("q", q_hbm, q_v), ("k", k_hbm, k_v), ("v", v_hbm, v_v),
            ("w", w_hbm, w_all.at[block(z)]), ("fisher", fisher_hbm, fisher_v),
        ):
            load(name, src, dst)

    def forward(h):
        span = pl.ds(h * HD, HD)
        scores = dot(k_v[:, span], q_v[:, span], NT) * scale
        shifted = jnp.where(u_segment == t_segment, scores, FLOOR_SCORE)
        largest = jnp.max(shifted, axis=0, keepdims=True)
        weights = jnp.exp(shifted - largest)
        probs = weights * (1.0 / jnp.sum(weights, axis=0, keepdims=True))
        probs_t[h] = probs
        attended = dot(v_v[:, span], probs.astype(BF16), TN)
        att_t[0, span, :] = jnp.where(t_position < filled, attended, 0.0).astype(BF16)

    def share_attended():
        for d in (1, 3, 2):
            send(f"a{d}", att_t.at[0], att_t.at[(NX - d) % NX], at(dx=d))

    def end_w():
        arrive("w+3B", "w-3A", "w+4A", "w-4B")
        locals_["w"].wait()

    def counts():
        arrive("c+4", "c-3")
        cnt[...] = sum(cnt_z[d] for d in range(NZ))
        for d in range(1, NX):
            send(f"cx{d}", cnt, cnt_x.at[d], at(dx=d))

    def grad_part(slot):
        term = dot(w_all[...], g_all[slot], TN)
        if slot == 0:
            x_own[...] = term
        else:
            xs[slot] = term.astype(BF16)
            send(f"r{slot}", xs.at[slot], xr.at[slot], at(dx=slot))

    def weight_part(offset, slots=range(NX), more=False):
        target = (z + offset + NZ) % NZ
        term = sum(dot(g_all[j, block(target), :], att_t[j], NT) for j in slots)
        if more:
            term = z_acc[offset % NZ] + term
        z_acc[offset % NZ] = term

    def sum_z(sign, step, name):
        first = 1 if (sign == "+") == (name[0] == "A") else 2
        offset = 5 - step if sign == "+" else step - 5
        cut = quarter_of(name)
        value = z_acc[offset % NZ, cut, :]
        mine = slot_of(sign, step, name)
        if step > first:
            arrive(f"z{sign}{step - 1}{name}")
            value = value + zr[slot_of(sign, step - 1, name)].astype(F32)
        zs[mine] = value.astype(BF16)
        send(f"z{sign}{step}{name}", zs.at[mine], zr.at[mine], at(dz=1 if sign == "+" else -1))

    quarter = rows // (2 * Q)

    def quarter_of(name):
        return pl.ds((Q * (name[0] == "B") + int(name[1])) * quarter, quarter)

    def slot_of(sign, step, name):
        return ((2 * (sign == "-") + (name[0] == "B")) * Q + int(name[1])) * 4 + step - 1

    def backward():
        all_of("r", xr.at[pl.ds(1, NX - 1)], "r").wait_recv()
        value = x_own[...]
        for j in (1, 3, 2):
            value = value + xr[j].astype(F32)
        grad_t[...] = jnp.where(t_position < filled, value, 0.0).astype(BF16)
        for h in range(heads):
            span = pl.ds(h * HD, HD)
            probs = probs_t[h]
            out_grad = grad_t[span, :]
            diagonal = jnp.sum(out_grad.astype(F32) * att_t[0, span, :].astype(F32), axis=0, keepdims=True)
            grad_probs = dot(v_v[:, span], out_grad, NN)
            grad_scores = (probs * (grad_probs - diagonal)).astype(BF16)
            gk_v[:, span] = (dot(grad_scores, q_v[:, span], NN) * scale).astype(BF16)
            gq_v[:, span] = (dot(grad_scores, k_v[:, span], TN) * scale).astype(BF16)
            gv_v[:, span] = dot(probs.astype(BF16), out_grad, NT).astype(BF16)

    def end_z():
        all_of("x", cnt_x.at[pl.ds(1, NX - 1)], "x").wait_recv()
        patches = cnt[...]
        for d in range(1, NX):
            patches = patches + cnt_x[d]
        inverse = 1.0 / patches[0:1, 0:1]
        locals_["fisher"].wait()
        for name in [part + str(j) for part in "BA" for j in range(Q)]:
            cut = quarter_of(name)
            value = z_acc[0, cut, :]
            for sign in "+-":
                arrive(f"z{sign}4{name}")
                value = value + zr[slot_of(sign, 4, name)].astype(F32)
            wg_v[cut, :] = value
            fn_v[cut, :] = fisher_v[cut, :] + value * value * inverse

    start()
    locals_["len"].wait()
    finish = []
    total = jnp.int32(0)
    for j in range(len_ref.shape[1]):
        total = total + len_ref[0, j]
        finish.append(total)
    filled = finish[-1]
    u_position = lax.broadcasted_iota(jnp.int32, (tokens, 1), 0)
    t_position = lax.broadcasted_iota(jnp.int32, (1, tokens), 1)
    u_segment = jnp.zeros((tokens, 1), jnp.int32)
    t_segment = jnp.zeros((1, tokens), jnp.int32)
    for end in finish:
        u_segment += (u_position >= end).astype(jnp.int32)
        t_segment += (t_position >= end).astype(jnp.int32)
    cnt_z[0] = jnp.full(cnt.shape, filled.astype(F32), F32)
    hand_count("+", 1)
    hand_count("-", 1)
    for name in ("q", "k", "v"):
        locals_[name].wait()
    for task in ORDER:
        if task[:3] == "fwd":
            forward(int(task[3]))
        elif task == "at":
            share_attended()
        elif task[:6] == "spread":
            spread(int(task[6]), int(task[7]))
        elif task[:2] == "ry":
            relay_y(int(task[2]), task[3], int(task[4]))
        elif task[:2] == "ey":
            end_y(int(task[2]), int(task[3]))
        elif task[:2] == "rw":
            relay_w(task[2], int(task[3]), task[4])
        elif task == "enda":
            all_of("a", att_t.at[pl.ds(1, NX - 1)], "a").wait_recv()
        elif task[:2] == "ec":
            end_core(int(task[2]))
        elif task == "c4":
            hand_count("+", 4)
        elif task == "cx":
            counts()
        elif task == "wt":
            end_w()
        elif task[:2] == "px":
            grad_part(int(task[2]))
        elif task == "pzp":
            weight_part(4, (0, 1, 3))
        elif task == "pzq":
            weight_part(4, (2,), True)
        elif task[:2] == "pz":
            weight_part(int(task[2:]))
        elif task[:2] == "sz":
            sum_z(task[2], int(task[3]), task[4:])
        elif task == "bwd":
            backward()
        else:
            end_z()

    blocks = (NX - 1) + NX * (2 + 1 + NY)
    for kind, ref in (
        ("w", w_all.at[pl.ds(0, len(senders["w"]) * half)]),
        ("c", cnt_z.at[pl.ds(0, len(senders["c"]))]),
        ("g", g_all.at[:, pl.ds(0, blocks * rows // NX)]),
        ("a", att_t.at[pl.ds(0, NX - 1)]),
        ("r", xs.at[pl.ds(0, NX - 1)]),
        ("x", cnt_x.at[pl.ds(0, NX - 1)]),
        ("z", zs.at[pl.ds(0, len(senders["z"]))]),
    ):
        all_of(kind, ref, "a").wait_send()


def copy_kernel(*refs):
    n = len(refs) // 2
    sem = refs[-1]
    copies = [pltpu.make_async_copy(refs[i], refs[n + i], sem.at[i]) for i in range(n)]
    for copy in copies:
        copy.start()
    for copy in copies:
        copy.wait()


def per_device(queries, keys, values, upstream, out_weight, fisher, image_lengths):
    tokens, width = queries.shape
    rows = out_weight.shape[0]
    heads = width // HD
    hbm = pl.BlockSpec(memory_space=pl.ANY)
    vm = pltpu.VMEM
    scratch = [
        vm((tokens, width), BF16),
        vm((tokens, width), BF16),
        vm((tokens, width), BF16),
        vm(upstream.shape, BF16),
        vm((rows, width), F32),
        vm((upstream.shape[1], tokens), BF16),
        vm((NX, NZ * rows, tokens), BF16),
        vm((NZ * rows, width), BF16),
        vm((NX, width, tokens), BF16),
        vm((heads, tokens, tokens), F32),
        vm((NX, width, tokens), BF16),
        vm((NX, width, tokens), BF16),
        vm((width, tokens), F32),
        vm((width, tokens), BF16),
        vm((16 * Q, rows // (2 * Q), width), BF16),
        vm((16 * Q, rows // (2 * Q), width), BF16),
        vm((NZ, rows, width), F32),
        vm((8, HD), F32),
        vm((NX, 8, HD), F32),
        vm((NZ, 8, HD), F32),
        pltpu.SMEM(image_lengths.shape, jnp.int32),
        pltpu.SemaphoreType.DMA((7,)),
        pltpu.SemaphoreType.DMA((N_REMOTE,)),
        pltpu.SemaphoreType.DMA((N_LOCAL,)),
    ]
    shapes = [((tokens, width), BF16)] * 3 + [((rows, width), F32)] * 2
    inputs = (image_lengths, queries, keys, values, upstream, out_weight, fisher)
    results = pl.pallas_call(
        kernel,
        out_shape=[pltpu.VMEM(*shape) for shape in shapes],
        in_specs=[hbm] * 7,
        out_specs=[pl.BlockSpec(memory_space=pltpu.VMEM)] * 5,
        scratch_shapes=scratch,
        compiler_params=pltpu.CompilerParams(
            collective_id=0, has_side_effects=True, vmem_limit_bytes=VMEM_LIMIT
        ),
    )(*(pltpu.with_memory_space_constraint(a, pltpu.HBM) for a in inputs))
    return pl.pallas_call(
        copy_kernel,
        out_shape=[pltpu.HBM(*shape) for shape in shapes],
        in_specs=[pl.BlockSpec(memory_space=pltpu.VMEM)] * 5,
        out_specs=[hbm] * 5,
        scratch_shapes=[pltpu.SemaphoreType.DMA((5,))],
        compiler_params=pltpu.CompilerParams(vmem_limit_bytes=VMEM_LIMIT),
    )(*(pltpu.with_memory_space_constraint(a, pltpu.VMEM) for a in results))


def solution(mesh):
    placed = P("dp", "tensor")
    return jax.shard_map(
        per_device,
        mesh=mesh,
        in_specs=(placed,) * 6 + (P("dp", None),),
        out_specs=(placed,) * 5,
        check_vma=False,
    )
```
